128 devices in a mesh: mem: 16 (over y, x_lo, core), space: 8 (over z, x_hi).
Axes of the slice: x: 4 (x_hi: 2, x_lo: 2; x = x_hi * 2 + x_lo), y: 4, z: 4, core: 2. Of those that a mesh axis runs over, the one named last changes fastest.
Arguments:
- members: bfloat16 [16, 137, 128, 1024], P('mem', None, 'space'), may hold values from -6 to 6
- increment: bfloat16 [137, 128, 1024], P(None, 'space'), may hold values from -6 to 6
- vertical: bfloat16 [137, 137], replicated, may hold values from -1 to 2
- spectral_weights: float32 [128, 1024], P(None, 'space'), may hold values from 0.05 to 1
- tile_rows: int32 [128], replicated, may hold values from 0 to 127, each once
Outputs:
- covariance_product: bfloat16 [137, 128, 1024], P(None, 'space')
The draws below stay inside these ranges and needn't reach their ends.
All inputs are finite; a program needn't handle non-finite values.
Results may differ from the reference program's by a relative error of at most 0.02.
Values may be sent and summed in bfloat16 or wider, within the bound.
No kernel may reach another device: no remote copies, remote signals or barrier semaphores. Data moves between devices by JAX's collectives and lax.ppermute only.
A program may use at most 128 MiB of HBM per device.

```python
import math
import jax
import jax.numpy as jnp
from jax import lax

LEV = 137
NX = 1024
NY = 128
MEMBERS = 16


def draw_vertical(key, part):
    key = jax.random.fold_in(key, 7)
    ranks = lax.broadcasted_iota(jnp.int32, (LEV, LEV), 0)
    others = lax.broadcasted_iota(jnp.int32, (LEV, LEV), 1)
    identity = (ranks == others).astype(jnp.float32)
    noise = jnp.clip(jax.random.normal(key, (LEV, LEV), jnp.float32), -4.0, 4.0)
    return (identity + noise * (0.5 / LEV ** 0.5)).astype(jnp.bfloat16)


def shard_levels(rng, shape, shards, low, high):
    loudness = 1.0
    for dim, shards_of in shards:
        draws = jax.random.uniform(jax.random.fold_in(jax.random.fold_in(rng, 6), dim), (shards_of,), jnp.float32, low / len(shards), high / len(shards))
        loudness = loudness * jnp.repeat(jnp.exp(draws), shape[dim] // shards_of).reshape((-1,) + (1,) * (len(shape) - 1 - dim))
    return loudness


def bell_draw(own_key, extent, deviation, most, shards=(), kind=jnp.bfloat16):
    level = shard_levels(own_key, extent, shards, -0.22, 0.18) if shards else 1.0
    values = jax.random.normal(own_key, extent, jnp.float32) * deviation * level
    return jnp.minimum(jnp.maximum(values, -most), most).astype(kind)


def setup_inputs(seed: int = 0) -> dict:
    key_of = jax.random.split(jax.random.key(seed), 6)
    members = bell_draw(key_of[0], (MEMBERS, LEV, NY, NX), 1.0, 6.0, ((0, 16), (2, 8)))
    increment = bell_draw(key_of[1], (LEV, NY, NX), 1.0, 6.0, ((1, 8),))
    vertical = draw_vertical(jax.random.fold_in(key_of[5], 71), 0)
    spectral_weights = jnp.clip(jnp.exp(math.log(1.0) - 2.9957323 * jax.random.uniform(key_of[3], (NY, NX), jnp.float32) ** shard_levels(key_of[3], (NY, NX), ((1, 8),), -0.2, 0.2)), 0.05, 1.0)
    tile_rows = jax.random.permutation(key_of[4], NY).astype(jnp.int32)
    return {"members": members, "increment": increment, "vertical": vertical, "spectral_weights": spectral_weights, "tile_rows": tile_rows}


root_two = 1.4142135623730951


def forward_real(field, axis):
    moved = jnp.moveaxis(field, axis, -1)
    length = moved.shape[-1]
    middle = length // 2
    spectrum = jnp.fft.rfft(moved, norm="ortho")
    real_part = spectrum.real
    imag_part = spectrum.imag
    packed = jnp.concatenate([real_part[..., :1], root_two * real_part[..., 1:middle], real_part[..., middle:middle + 1], -root_two * imag_part[..., 1:middle]], axis=-1)
    return jnp.moveaxis(packed, -1, axis)


def backward_real(packed, axis):
    moved = jnp.moveaxis(packed, axis, -1)
    length = moved.shape[-1]
    middle = length // 2
    cosines = moved[..., :middle + 1]
    sines = moved[..., middle + 1:]
    edge_zero = jnp.zeros_like(moved[..., :1])
    real_part = jnp.concatenate([cosines[..., :1], cosines[..., 1:middle] / root_two, cosines[..., middle:]], axis=-1)
    imag_part = jnp.concatenate([edge_zero, -sines / root_two, edge_zero], axis=-1)
    field = jnp.fft.irfft(real_part + 1j * imag_part, n=length, norm="ortho")
    return jnp.moveaxis(field, -1, axis)


def reference(members, increment, vertical, spectral_weights, tile_rows):
    inverse = jnp.argsort(tile_rows).astype(jnp.int32)

    def add_member(summed, member):
        product = (member.astype(jnp.float32) * increment.astype(jnp.float32)).astype(jnp.bfloat16)
        localized = jnp.dot(vertical, product.reshape(LEV, -1), preferred_element_type=jnp.float32)
        localized = localized.astype(jnp.bfloat16).reshape(LEV, NY, NX)
        coeffs = forward_real(localized.astype(jnp.float32), 2).astype(jnp.bfloat16)
        grid_order = jnp.take(coeffs, inverse, axis=1).astype(jnp.float32)
        spectral = forward_real(grid_order, 1)
        damped = (spectral * spectral_weights[None]).astype(jnp.bfloat16)
        returned = jnp.take(backward_real(damped.astype(jnp.float32), 1), tile_rows, axis=1).astype(jnp.bfloat16)
        gridded = backward_real(returned.astype(jnp.float32), 2)
        return summed + member.astype(jnp.float32) * gridded, None

    summed, unused = lax.scan(add_member, jnp.zeros((LEV, NY, NX), jnp.float32), members)
    return summed.astype(jnp.bfloat16)
```

```python
import functools
import math

import jax
import jax.numpy as jnp
import numpy as np
from jax import lax
from jax.experimental import pallas as pl
from jax.experimental.pallas import tpu as pltpu
from jax.sharding import PartitionSpec as P

BF16, F32 = jnp.bfloat16, jnp.float32
LANES = 128
VMEM_LIMIT = 48 * 1024 * 1024
CHUNKS = (32, 32, 32, 32, 9)
STEP = 8


def wave_table(length):
    ranks = np.arange(length)[:, None]
    middle = length // 2
    wavenumber = np.where(ranks <= middle, ranks, ranks - middle)
    angles = wavenumber * np.arange(length)[None, :] % length * (2.0 * math.pi / length)
    edge, inner = 1.0 / math.sqrt(length), math.sqrt(2.0 / length)
    values = np.where(
        ranks == 0,
        edge,
        np.where(
            ranks < middle,
            inner * np.cos(angles),
            np.where(ranks == middle, edge * np.cos(angles), inner * np.sin(angles)),
        ),
    )
    return values.astype(jnp.bfloat16)


def params():
    return pltpu.CompilerParams(vmem_limit_bytes=VMEM_LIMIT)


def mix_kernel(vertical_ref, member_ref, increment_ref, *refs):
    *out_refs, rows, mixed = refs
    levels, stored, _ = member_ref.shape
    tiles = rows.shape[0]
    product = member_ref[...].astype(F32) * increment_ref[...].astype(F32)
    product = product.reshape(levels * stored, tiles * LANES)
    for t in range(tiles):
        rows[t] = product[:, t * LANES : (t + 1) * LANES]
    vertical = vertical_ref[...]
    for p in range(stored):
        at = pl.ds(p, levels, stride=stored)
        block = jnp.concatenate([rows[t, at, :] for t in range(tiles)], axis=1).astype(BF16)
        block = jnp.dot(vertical, block, preferred_element_type=F32)
        for t in range(tiles):
            mixed[t, at, :] = block[:, t * LANES : (t + 1) * LANES]
    start = 0
    for out_ref in out_refs:
        size = out_ref.shape[0]
        for t in range(tiles):
            part = mixed[t, start * stored : (start + size) * stored, :].astype(BF16)
            out_ref[:, :, t * LANES : (t + 1) * LANES] = part.reshape(size, stored, LANES)
        start += size


def mix(vertical, member, increment, chunks, width=256):
    levels, stored, columns = member.shape
    wide = lambda size: pl.BlockSpec((size, stored, width), lambda i: (0, 0, i))
    return pl.pallas_call(
        mix_kernel,
        grid=(columns // width,),
        in_specs=[pl.BlockSpec((levels, levels), lambda i: (0, 0)), wide(levels), wide(levels)],
        out_specs=[wide(size) for size in chunks],
        out_shape=[jax.ShapeDtypeStruct((size, stored, columns), BF16) for size in chunks],
        scratch_shapes=[pltpu.VMEM((width // LANES, levels * stored, LANES), F32)] * 2,
        compiler_params=params(),
        name="mix",
    )(vertical, member, increment)


def forward_kernel(basis_ref, x_ref, out_ref):
    size, stored, columns = x_ref.shape
    parts, _, _, width = out_ref.shape
    coeffs = jnp.dot(
        x_ref[...].reshape(size * stored, columns), basis_ref[...], preferred_element_type=F32
    ).astype(BF16)
    for s in range(parts):
        out_ref[s] = coeffs[:, s * width : (s + 1) * width].reshape(size, stored, width)


def forward(basis, x, parts):
    size, stored, columns = x.shape
    width = columns // parts
    step = min(STEP, size)
    return pl.pallas_call(
        forward_kernel,
        grid=(pl.cdiv(size, step),),
        in_specs=[
            pl.BlockSpec((columns, columns), lambda i: (0, 0)),
            pl.BlockSpec((step, stored, columns), lambda i: (i, 0, 0)),
        ],
        out_specs=pl.BlockSpec((parts, step, stored, width), lambda i: (0, i, 0, 0)),
        out_shape=jax.ShapeDtypeStruct((parts, size, stored, width), BF16),
        compiler_params=params(),
        cost_estimate=pl.CostEstimate(
            flops=2 * size * stored * columns * columns,
            bytes_accessed=2 * (2 * x.size + basis.size),
            transcendentals=0,
        ),
        name="forward",
    )(basis, x)


def filter_kernel(basis_ref, basis_t_ref, weights_ref, x_ref, out_ref):
    parts, step, stored, width = x_ref.shape
    rows = parts * stored
    x = jnp.concatenate([x_ref[:, l].reshape(rows, width) for l in range(step)], axis=1)
    spectral = jnp.dot(basis_ref[...], x, preferred_element_type=F32)
    weights = jnp.concatenate([weights_ref[...]] * step, axis=1)
    damped = (spectral * weights).astype(BF16)
    back = jnp.dot(basis_t_ref[...], damped, preferred_element_type=F32).astype(BF16)
    for l in range(step):
        out_ref[:, l] = back[:, l * width : (l + 1) * width].reshape(parts, stored, width)


def filter_rows(basis, basis_t, weights, x):
    parts, size, stored, width = x.shape
    rows = parts * stored
    step = min(STEP, size)
    whole = lambda a: pl.BlockSpec(a.shape, lambda i: (0, 0))
    block = pl.BlockSpec((parts, step, stored, width), lambda i: (0, i, 0, 0))
    return pl.pallas_call(
        filter_kernel,
        grid=(pl.cdiv(size, step),),
        in_specs=[whole(basis), whole(basis_t), whole(weights), block],
        out_specs=block,
        out_shape=jax.ShapeDtypeStruct(x.shape, BF16),
        compiler_params=params(),
        cost_estimate=pl.CostEstimate(
            flops=4 * rows * x.size, bytes_accessed=4 * x.size, transcendentals=0
        ),
        name="filter",
    )(basis, basis_t, weights, x)


def backward_kernel(basis_ref, member_ref, x_ref, out_ref):
    parts, step, stored, width = x_ref.shape
    x = jnp.concatenate([x_ref[s].reshape(step * stored, width) for s in range(parts)], axis=1)
    gridded = jnp.dot(x, basis_ref[...], preferred_element_type=F32)
    member = member_ref[...].astype(F32).reshape(gridded.shape)
    out_ref[...] = (member * gridded).astype(BF16).reshape(out_ref.shape)


def backward(basis, member, x, start):
    parts, size, stored, width = x.shape
    columns = parts * width
    step = min(STEP, size)
    first = start // step
    assert first * step == start
    return pl.pallas_call(
        backward_kernel,
        grid=(pl.cdiv(size, step),),
        in_specs=[
            pl.BlockSpec((columns, columns), lambda i: (0, 0)),
            pl.BlockSpec((step, stored, columns), lambda i: (first + i, 0, 0)),
            pl.BlockSpec((parts, step, stored, width), lambda i: (0, i, 0, 0)),
        ],
        out_specs=pl.BlockSpec((step, stored, columns), lambda i: (i, 0, 0)),
        out_shape=jax.ShapeDtypeStruct((size, stored, columns), BF16),
        compiler_params=params(),
        cost_estimate=pl.CostEstimate(
            flops=2 * x.size * columns,
            bytes_accessed=2 * (3 * x.size + basis.size),
            transcendentals=0,
        ),
        name="backward",
    )(basis, member, x)


def shards(spaces, mems, members, increment, vertical, spectral_weights, tile_rows):
    levels, stored, columns = increment.shape
    member = members[0]
    table = wave_table(columns)
    basis_x, basis_xt = jnp.asarray(table), jnp.asarray(np.ascontiguousarray(table.T))
    rows = tile_rows.shape[0]
    chosen = (lax.broadcasted_iota(jnp.int32, (rows, rows), 0) == tile_rows[None, :]).astype(BF16)
    basis_y = jnp.dot(jnp.asarray(wave_table(rows)), chosen, preferred_element_type=F32).astype(BF16)
    basis_yt = basis_y.T
    localized = mix(vertical, member, increment, CHUNKS)
    out = jnp.zeros((levels, stored, columns), BF16)
    start = 0
    for chunk in localized:
        size = chunk.shape[0]
        coeffs = forward(basis_xt, chunk, spaces)
        coeffs = lax.all_to_all(coeffs, "space", 0, 0, tiled=True)
        returned = filter_rows(basis_y, basis_yt, spectral_weights, coeffs)
        returned = lax.all_to_all(returned, "space", 0, 0, tiled=True)
        part = backward(basis_x, member, returned, start)
        full = -(-size // 16) * 16
        part = jnp.pad(part, ((0, full - size), (0, 0), (0, 0)))
        part = lax.psum_scatter(
            part.reshape(full * stored, columns), "mem", scatter_dimension=0, tiled=True
        )
        part = lax.all_gather(part, "mem", axis=0, tiled=True)
        part = part[: size * stored].reshape(size, stored, columns)
        out = lax.dynamic_update_slice(out, part, (start, 0, 0))
        start += size
    return out


def solution(mesh):
    return jax.shard_map(
        functools.partial(shards, mesh.shape["space"], mesh.shape["mem"]),
        mesh=mesh,
        in_specs=(
            P("mem", None, "space", None),
            P(None, "space", None),
            P(),
            P(None, "space"),
            P(),
        ),
        out_specs=P(None, "space", None),
        check_vma=False,
    )
```

```python
import math

import jax
import jax.numpy as jnp
import numpy as np
from jax import lax
from jax.experimental import pallas as pl
from jax.experimental.pallas import tpu as pltpu
from jax.sharding import PartitionSpec as P

BF16, F32 = jnp.bfloat16, jnp.float32
LANES = 128
VMEM_LIMIT = 48 * 1024 * 1024
CHUNKS = (46, 46, 45)
STEP = 23


def wave_table(length):
    ranks = np.arange(length)[:, None]
    middle = length // 2
    wavenumber = np.where(ranks <= middle, ranks, ranks - middle)
    angles = wavenumber * np.arange(length)[None, :] % length * (2.0 * math.pi / length)
    edge, inner = 1.0 / math.sqrt(length), math.sqrt(2.0 / length)
    values = np.where(
        ranks == 0,
        edge,
        np.where(
            ranks < middle,
            inner * np.cos(angles),
            np.where(ranks == middle, edge * np.cos(angles), inner * np.sin(angles)),
        ),
    )
    return values.astype(jnp.bfloat16)


def params():
    return pltpu.CompilerParams(vmem_limit_bytes=VMEM_LIMIT)


def mix_kernel(vertical_ref, member_ref, increment_ref, *refs):
    *out_refs, rows, mixed = refs
    levels, stored, _ = member_ref.shape
    tiles = rows.shape[0]
    product = member_ref[...].astype(F32) * increment_ref[...].astype(F32)
    product = product.reshape(levels * stored, tiles * LANES)
    for t in range(tiles):
        rows[t] = product[:, t * LANES : (t + 1) * LANES]
    vertical = vertical_ref[...]
    for p in range(stored):
        at = pl.ds(p, levels, stride=stored)
        block = jnp.concatenate([rows[t, at, :] for t in range(tiles)], axis=1).astype(BF16)
        block = jnp.dot(vertical, block, preferred_element_type=F32)
        for t in range(tiles):
            mixed[t, at, :] = block[:, t * LANES : (t + 1) * LANES]
    start = 0
    for out_ref in out_refs:
        size = out_ref.shape[0]
        for t in range(tiles):
            part = mixed[t, start * stored : (start + size) * stored, :].astype(BF16)
            out_ref[:, :, t * LANES : (t + 1) * LANES] = part.reshape(size, stored, LANES)
        start += size


def mix(vertical, member, increment, chunks, width=256):
    levels, stored, columns = member.shape
    wide = lambda size: pl.BlockSpec((size, stored, width), lambda i: (0, 0, i))
    return pl.pallas_call(
        mix_kernel,
        grid=(columns // width,),
        in_specs=[pl.BlockSpec((levels, levels), lambda i: (0, 0)), wide(levels), wide(levels)],
        out_specs=[wide(size) for size in chunks],
        out_shape=[jax.ShapeDtypeStruct((size, stored, columns), BF16) for size in chunks],
        scratch_shapes=[pltpu.VMEM((width // LANES, levels * stored, LANES), F32)] * 2,
        compiler_params=params(),
        name="mix",
    )(vertical, member, increment)


def cost(flops, values):
    return pl.CostEstimate(flops=flops, bytes_accessed=2 * values, transcendentals=0)


def at_tile(tile):
    return pl.ds(pl.multiple_of(tile * LANES, LANES), LANES)


def forward_kernel(order_ref, basis_ref, x_ref, *refs):
    *out_refs, coeffs = refs
    step, stored, columns = x_ref.shape
    coeffs[...] = jnp.dot(
        x_ref[...].reshape(step * stored, columns), basis_ref[...], preferred_element_type=F32
    ).astype(BF16)
    for d, out_ref in enumerate(out_refs):
        out_ref[...] = coeffs[:, at_tile(order_ref[d])].reshape(out_ref.shape)


def forward(order, basis, x):
    size, stored, columns = x.shape
    parts = columns // LANES
    step = min(STEP, size)
    piece = pl.BlockSpec((step, stored, LANES), lambda i, *_: (i, 0, 0))
    return pl.pallas_call(
        forward_kernel,
        grid_spec=pltpu.PrefetchScalarGridSpec(
            num_scalar_prefetch=1,
            grid=(pl.cdiv(size, step),),
            in_specs=[
                pl.BlockSpec((columns, columns), lambda i, *_: (0, 0)),
                pl.BlockSpec((step, stored, columns), lambda i, *_: (i, 0, 0)),
            ],
            out_specs=[piece] * parts,
            scratch_shapes=[pltpu.VMEM((step * stored, columns), BF16)],
        ),
        out_shape=[jax.ShapeDtypeStruct((size, stored, LANES), BF16)] * parts,
        compiler_params=params(),
        cost_estimate=cost(2 * x.size * columns, 2 * x.size + basis.size),
        name="forward",
    )(order, basis, x)


def filter_kernel(basis_ref, basis_t_ref, weights_ref, *refs):
    parts = len(refs) // 2
    x_refs, out_refs = refs[:parts], refs[parts:]
    step, stored, width = x_refs[0].shape
    x = jnp.concatenate(
        [jnp.concatenate([r[l] for r in x_refs], axis=0) for l in range(step)], axis=1
    )
    spectral = jnp.dot(basis_ref[...], x, preferred_element_type=F32)
    weights = jnp.concatenate([weights_ref[...]] * step, axis=1)
    damped = (spectral * weights).astype(BF16)
    back = jnp.dot(basis_t_ref[...], damped, preferred_element_type=F32).astype(BF16)
    for l in range(step):
        for d, out_ref in enumerate(out_refs):
            out_ref[l] = back[d * stored : (d + 1) * stored, l * width : (l + 1) * width]


def filter_rows(basis, basis_t, weights, pieces):
    parts = len(pieces)
    size, stored, width = pieces[0].shape
    step = min(STEP, size)
    whole = lambda a: pl.BlockSpec(a.shape, lambda i: (0, 0))
    block = pl.BlockSpec((step, stored, width), lambda i: (i, 0, 0))
    total = parts * pieces[0].size
    return pl.pallas_call(
        filter_kernel,
        grid=(pl.cdiv(size, step),),
        in_specs=[whole(basis), whole(basis_t), whole(weights)] + [block] * parts,
        out_specs=[block] * parts,
        out_shape=[jax.ShapeDtypeStruct(pieces[0].shape, BF16)] * parts,
        compiler_params=params(),
        cost_estimate=cost(4 * parts * stored * total, 2 * total),
        name="filter",
    )(basis, basis_t, weights, *pieces)


def backward_kernel(order_ref, tiles_ref, basis_ref, member_ref, *refs):
    *x_refs, keep_ref, give_ref, coeffs, held = refs
    step, stored, width = x_refs[0].shape
    for d, x_ref in enumerate(x_refs):
        coeffs[:, at_tile(order_ref[d])] = x_ref[...].reshape(step * stored, width)
    gridded = jnp.dot(coeffs[...], basis_ref[...], preferred_element_type=F32)
    held[...] = (member_ref[...].astype(F32).reshape(gridded.shape) * gridded).astype(BF16)
    half = len(x_refs) // 2
    for q in range(half):
        keep_ref[q] = held[:, at_tile(tiles_ref[q])].reshape(step, stored, width)
        give_ref[q] = held[:, at_tile(tiles_ref[half + q])].reshape(step, stored, width)


def backward(order, tiles, basis, member, pieces, start):
    parts = len(pieces)
    size, stored, width = pieces[0].shape
    columns = parts * width
    step = min(STEP, size)
    first = start // step
    assert first * step == start
    half = pl.BlockSpec((parts // 2, step, stored, width), lambda i, *_: (0, i, 0, 0))
    total = parts * pieces[0].size
    return pl.pallas_call(
        backward_kernel,
        grid_spec=pltpu.PrefetchScalarGridSpec(
            num_scalar_prefetch=2,
            grid=(pl.cdiv(size, step),),
            in_specs=[
                pl.BlockSpec((columns, columns), lambda i, *_: (0, 0)),
                pl.BlockSpec((step, stored, columns), lambda i, *_: (first + i, 0, 0)),
            ]
            + [pl.BlockSpec((step, stored, width), lambda i, *_: (i, 0, 0))] * parts,
            out_specs=[half] * 2,
            scratch_shapes=[pltpu.VMEM((step * stored, columns), BF16)] * 2,
        ),
        out_shape=[jax.ShapeDtypeStruct((parts // 2, size, stored, width), BF16)] * 2,
        compiler_params=params(),
        cost_estimate=cost(2 * total * columns, 3 * total + basis.size),
        name="backward",
    )(order, tiles, basis, member, *pieces)


def pair_kernel(a_ref, b_ref, *out_refs):
    for q, out_ref in enumerate(out_refs):
        out_ref[...] = (a_ref[q].astype(F32) + b_ref[q].astype(F32)).astype(BF16)


def pair_sum(a, b):
    parts, size, stored, width = a.shape
    step = min(STEP, size)
    block = pl.BlockSpec((parts, step, stored, width), lambda i: (0, i, 0, 0))
    return pl.pallas_call(
        pair_kernel,
        grid=(pl.cdiv(size, step),),
        in_specs=[block] * 2,
        out_specs=[pl.BlockSpec((step, stored, width), lambda i: (i, 0, 0))] * parts,
        out_shape=[jax.ShapeDtypeStruct(a.shape[1:], BF16)] * parts,
        compiler_params=params(),
        cost_estimate=cost(a.size, 3 * a.size),
        name="pair_sum",
    )(a, b)


def place_kernel(tiles_ref, mine_ref, theirs_ref, *refs):
    out_ref = refs[-1]
    half = mine_ref.shape[0]
    for q in range(half):
        out_ref[:, :, at_tile(tiles_ref[q])] = mine_ref[q]
        out_ref[:, :, at_tile(tiles_ref[half + q])] = theirs_ref[q]


def place(tiles, mine, theirs, out, start, levels):
    half, size, stored, width = mine.shape
    columns = 2 * half * width
    step = min(STEP, size)
    first = start // step
    block = pl.BlockSpec((half, step, stored, width), lambda i, *_: (0, i, 0, 0))
    held = [] if out is None else [out]
    return pl.pallas_call(
        place_kernel,
        grid_spec=pltpu.PrefetchScalarGridSpec(
            num_scalar_prefetch=1,
            grid=(pl.cdiv(size, step),),
            in_specs=[block] * 2 + [pl.BlockSpec(memory_space=pl.ANY)] * len(held),
            out_specs=pl.BlockSpec((step, stored, columns), lambda i, *_: (first + i, 0, 0)),
        ),
        out_shape=jax.ShapeDtypeStruct((levels, stored, columns), BF16),
        input_output_aliases={3: 0} if held else {},
        compiler_params=params(),
        cost_estimate=cost(0, 4 * mine.size),
        name="place",
    )(tiles, mine, theirs, *held)


Y, XLO, CORE, Z, XHI = 4, 2, 2, 4, 2


def space_to(dz, dx):
    return [(z * XHI + x, (z + dz) % Z * XHI + (x ^ dx)) for z in range(Z) for x in range(XHI)]


def mem_to(dy, dx, dc):
    return [
        ((y * XLO + x) * CORE + c, ((y + dy) % Y * XLO + (x ^ dx)) * CORE + (c ^ dc))
        for y in range(Y)
        for x in range(XLO)
        for c in range(CORE)
    ]


HOPS = [(dz, dx) for dz in range(Z) for dx in range(XHI)]


def exchange(pieces):
    out = [None] * len(HOPS)
    for d, (dz, dx) in enumerate(HOPS):
        source = HOPS.index((-dz % Z, dx))
        out[source] = pieces[d] if d == 0 else lax.ppermute(pieces[d], "space", space_to(dz, dx))
    return out


def add(*terms):
    return sum(t.astype(F32) for t in terms).astype(BF16)


def shards(members, increment, vertical, spectral_weights, tile_rows):
    levels, stored, columns = increment.shape
    member = members[0]
    table = wave_table(columns)
    basis_x, basis_xt = jnp.asarray(table), jnp.asarray(np.ascontiguousarray(table.T))
    space, mem = lax.axis_index("space"), lax.axis_index("mem")
    z, x, y, core = space // XHI, space % XHI, mem // (XLO * CORE), mem % CORE
    order = jnp.stack([(z + dz) % Z * XHI + (x ^ dx) for dz, dx in HOPS]).astype(jnp.int32)
    tiles = jnp.stack(
        [(core ^ dc) * Y + (y + dy) % Y for dc in range(CORE) for dy in range(Y)]
    ).astype(jnp.int32)
    rows = tile_rows.shape[0]
    held = jnp.take(tile_rows.reshape(len(HOPS), stored), order, axis=0).reshape(1, rows)
    chosen = (lax.broadcasted_iota(jnp.int32, (rows, rows), 0) == held).astype(BF16)
    basis_y = jnp.dot(jnp.asarray(wave_table(rows)), chosen, preferred_element_type=F32).astype(BF16)
    basis_yt = basis_y.T
    localized = mix(vertical, member, increment, CHUNKS)
    out = None
    start = 0
    for chunk in localized:
        size = chunk.shape[0]
        pieces = exchange(forward(order, basis_xt, chunk))
        pieces = exchange(filter_rows(basis_y, basis_yt, spectral_weights, pieces))
        keep, give = backward(order, tiles, basis_x, member, pieces, start)
        keep = pair_sum(keep, lax.ppermute(give, "mem", mem_to(0, 0, 1)))
        part = add(
            keep[0], *[lax.ppermute(keep[dy], "mem", mem_to(dy, 0, 0)) for dy in range(1, Y)]
        )
        part = add(part, lax.ppermute(part, "mem", mem_to(0, 1, 0)))
        mine = jnp.stack(
            [part] + [lax.ppermute(part, "mem", mem_to(-dy, 0, 0)) for dy in range(1, Y)]
        )
        theirs = lax.ppermute(mine, "mem", mem_to(0, 0, 1))
        out = place(tiles, mine, theirs, out, start, levels)
        start += size
    return out


def solution(mesh):
    return jax.shard_map(
        shards,
        mesh=mesh,
        in_specs=(
            P("mem", None, "space", None),
            P(None, "space", None),
            P(),
            P(None, "space"),
            P(),
        ),
        out_specs=P(None, "space", None),
        check_vma=False,
    )
```

```python
import math

import jax
import jax.numpy as jnp
import numpy as np
from jax import lax
from jax.experimental import pallas as pl
from jax.experimental.pallas import tpu as pltpu
from jax.sharding import PartitionSpec as P

BF16, F32 = jnp.bfloat16, jnp.float32
LANES = 128
VMEM_LIMIT = 20 * 1024 * 1024
CHUNKS = (46, 46, 45)
STEP = 23


def wave_table(length):
    ranks = np.arange(length)[:, None]
    middle = length // 2
    wavenumber = np.where(ranks <= middle, ranks, ranks - middle)
    angles = wavenumber * np.arange(length)[None, :] % length * (2.0 * math.pi / length)
    edge, inner = 1.0 / math.sqrt(length), math.sqrt(2.0 / length)
    values = np.where(
        ranks == 0,
        edge,
        np.where(
            ranks < middle,
            inner * np.cos(angles),
            np.where(ranks == middle, edge * np.cos(angles), inner * np.sin(angles)),
        ),
    )
    return values.astype(jnp.bfloat16)


def params():
    return pltpu.CompilerParams(vmem_limit_bytes=VMEM_LIMIT)


def mix_kernel(vertical_ref, member_ref, increment_ref, *refs):
    *out_refs, rows, mixed = refs
    levels, stored, _ = member_ref.shape
    tiles = rows.shape[0]
    product = member_ref[...].astype(F32) * increment_ref[...].astype(F32)
    product = product.reshape(levels * stored, tiles * LANES)
    for t in range(tiles):
        rows[t] = product[:, t * LANES : (t + 1) * LANES]
    vertical = vertical_ref[...]
    for p in range(stored):
        at = pl.ds(p, levels, stride=stored)
        block = jnp.concatenate([rows[t, at, :] for t in range(tiles)], axis=1).astype(BF16)
        block = jnp.dot(vertical, block, preferred_element_type=F32)
        for t in range(tiles):
            mixed[t, at, :] = block[:, t * LANES : (t + 1) * LANES]
    start = 0
    for out_ref in out_refs:
        size = out_ref.shape[0]
        for t in range(tiles):
            part = mixed[t, start * stored : (start + size) * stored, :].astype(BF16)
            out_ref[:, :, t * LANES : (t + 1) * LANES] = part.reshape(size, stored, LANES)
        start += size


def mix(vertical, member, increment, chunks, width=256):
    levels, stored, columns = member.shape
    wide = lambda size: pl.BlockSpec((size, stored, width), lambda i: (0, 0, i))
    return pl.pallas_call(
        mix_kernel,
        grid=(columns // width,),
        in_specs=[pl.BlockSpec((levels, levels), lambda i: (0, 0)), wide(levels), wide(levels)],
        out_specs=[wide(size) for size in chunks],
        out_shape=[jax.ShapeDtypeStruct((size, stored, columns), BF16) for size in chunks],
        scratch_shapes=[pltpu.VMEM((width // LANES, levels * stored, LANES), F32)] * 2,
        compiler_params=params(),
        name="mix",
    )(vertical, *[pltpu.with_memory_space_constraint(a, pltpu.HBM) for a in (member, increment)])


def cost(flops, values):
    return pl.CostEstimate(flops=flops, bytes_accessed=2 * values, transcendentals=0)


def at_tile(tile):
    return pl.ds(pl.multiple_of(tile * LANES, LANES), LANES)


def forward_kernel(basis_ref, x_ref, out_ref):
    step, stored, columns = x_ref.shape
    coeffs = jnp.dot(
        x_ref[...].reshape(step * stored, columns), basis_ref[...], preferred_element_type=F32
    ).astype(BF16)
    for d in range(out_ref.shape[0]):
        out_ref[d] = coeffs[:, d * LANES : (d + 1) * LANES].reshape(step, stored, LANES)


def forward(basis, x):
    size, stored, columns = x.shape
    parts = columns // LANES
    step = min(STEP, size)
    return pl.pallas_call(
        forward_kernel,
        grid=(pl.cdiv(size, step),),
        in_specs=[
            pl.BlockSpec((columns, columns), lambda i: (0, 0)),
            pl.BlockSpec((step, stored, columns), lambda i: (i, 0, 0)),
        ],
        out_specs=pl.BlockSpec((parts, step, stored, LANES), lambda i: (0, i, 0, 0)),
        out_shape=jax.ShapeDtypeStruct((parts, size, stored, LANES), BF16),
        compiler_params=params(),
        cost_estimate=cost(2 * x.size * columns, 2 * x.size + basis.size),
        name="forward",
    )(basis, x)


def filter_kernel(basis_ref, basis_t_ref, weights_ref, x_ref, out_ref):
    parts, step, stored, width = x_ref.shape
    x = jnp.concatenate([x_ref[:, l].reshape(parts * stored, width) for l in range(step)], axis=1)
    spectral = jnp.dot(basis_ref[...], x, preferred_element_type=F32)
    weights = jnp.concatenate([weights_ref[...]] * step, axis=1)
    damped = (spectral * weights).astype(BF16)
    back = jnp.dot(basis_t_ref[...], damped, preferred_element_type=F32).astype(BF16)
    for l in range(step):
        out_ref[:, l] = back[:, l * width : (l + 1) * width].reshape(parts, stored, width)


def filter_rows(basis, basis_t, weights, x):
    parts, size, stored, width = x.shape
    step = min(STEP, size)
    whole = lambda a: pl.BlockSpec(a.shape, lambda i: (0, 0))
    block = pl.BlockSpec((parts, step, stored, width), lambda i: (0, i, 0, 0))
    return pl.pallas_call(
        filter_kernel,
        grid=(pl.cdiv(size, step),),
        in_specs=[whole(basis), whole(basis_t), whole(weights), block],
        out_specs=block,
        out_shape=jax.ShapeDtypeStruct(x.shape, BF16),
        compiler_params=params(),
        cost_estimate=cost(4 * parts * stored * x.size, 2 * x.size),
        name="filter",
    )(basis, basis_t, weights, x)


def backward_kernel(tiles_ref, basis_ref, member_ref, x_ref, keep_ref, give_ref, held):
    parts, step, stored, width = x_ref.shape
    x = jnp.concatenate([x_ref[d].reshape(step * stored, width) for d in range(parts)], axis=1)
    gridded = jnp.dot(x, basis_ref[...], preferred_element_type=F32)
    held[...] = (member_ref[...].astype(F32).reshape(gridded.shape) * gridded).astype(BF16)
    half = parts // 2
    for q in range(half):
        keep_ref[q] = held[:, at_tile(tiles_ref[q])].reshape(step, stored, width)
        give_ref[q] = held[:, at_tile(tiles_ref[half + q])].reshape(step, stored, width)


def backward(tiles, basis, member, x, start):
    parts, size, stored, width = x.shape
    columns = parts * width
    step = min(STEP, size)
    first = start // step
    assert first * step == start
    half = pl.BlockSpec((parts // 2, step, stored, width), lambda i, *_: (0, i, 0, 0))
    total = x.size
    return pl.pallas_call(
        backward_kernel,
        grid_spec=pltpu.PrefetchScalarGridSpec(
            num_scalar_prefetch=1,
            grid=(pl.cdiv(size, step),),
            in_specs=[
                pl.BlockSpec((columns, columns), lambda i, *_: (0, 0)),
                pl.BlockSpec((step, stored, columns), lambda i, *_: (first + i, 0, 0)),
                pl.BlockSpec((parts, step, stored, width), lambda i, *_: (0, i, 0, 0)),
            ],
            out_specs=[half] * 2,
            scratch_shapes=[pltpu.VMEM((step * stored, columns), BF16)],
        ),
        out_shape=[jax.ShapeDtypeStruct((parts // 2, size, stored, width), BF16)] * 2,
        compiler_params=params(),
        cost_estimate=cost(2 * total * columns, 3 * total + basis.size),
        name="backward",
    )(tiles, basis, pltpu.with_memory_space_constraint(member, pltpu.HBM), x)


def pair_kernel(a_ref, b_ref, *out_refs):
    for q, out_ref in enumerate(out_refs):
        out_ref[...] = (a_ref[q].astype(F32) + b_ref[q].astype(F32)).astype(BF16)


def pair_sum(a, b):
    parts, size, stored, width = a.shape
    step = min(STEP, size)
    block = pl.BlockSpec((parts, step, stored, width), lambda i: (0, i, 0, 0))
    return pl.pallas_call(
        pair_kernel,
        grid=(pl.cdiv(size, step),),
        in_specs=[block] * 2,
        out_specs=[pl.BlockSpec((step, stored, width), lambda i: (i, 0, 0))] * parts,
        out_shape=[jax.ShapeDtypeStruct(a.shape[1:], BF16)] * parts,
        compiler_params=params(),
        cost_estimate=cost(a.size, 3 * a.size),
        name="pair_sum",
    )(a, b)


def place_kernel(tiles_ref, mine_ref, theirs_ref, *refs):
    out_ref = refs[-1]
    half = mine_ref.shape[0]
    for q in range(half):
        out_ref[:, :, at_tile(tiles_ref[q])] = mine_ref[q]
        out_ref[:, :, at_tile(tiles_ref[half + q])] = theirs_ref[q]


def place(tiles, mine, theirs, out, start, levels):
    half, size, stored, width = mine.shape
    columns = 2 * half * width
    step = min(STEP, size)
    first = start // step
    block = pl.BlockSpec((half, step, stored, width), lambda i, *_: (0, i, 0, 0))
    held = [] if out is None else [out]
    return pl.pallas_call(
        place_kernel,
        grid_spec=pltpu.PrefetchScalarGridSpec(
            num_scalar_prefetch=1,
            grid=(pl.cdiv(size, step),),
            in_specs=[block] * 2 + [pl.BlockSpec(memory_space=pl.ANY)] * len(held),
            out_specs=pl.BlockSpec((step, stored, columns), lambda i, *_: (first + i, 0, 0)),
        ),
        out_shape=jax.ShapeDtypeStruct((levels, stored, columns), BF16),
        input_output_aliases={3: 0} if held else {},
        compiler_params=params(),
        cost_estimate=cost(0, 4 * mine.size),
        name="place",
    )(tiles, mine, theirs, *held)


Y, XLO, CORE, Z, XHI = 4, 2, 2, 4, 2


def space_to(dz, dx):
    return [(z * XHI + x, (z + dz) % Z * XHI + (x ^ dx)) for z in range(Z) for x in range(XHI)]


def mem_to(dy, dx, dc):
    return [
        ((y * XLO + x) * CORE + c, ((y + dy) % Y * XLO + (x ^ dx)) * CORE + (c ^ dc))
        for y in range(Y)
        for x in range(XLO)
        for c in range(CORE)
    ]


def swap(pieces):
    return lax.all_to_all(pieces, "space", 0, 0, tiled=True)


tie = lax.optimization_barrier


def add(*terms):
    return sum(t.astype(F32) for t in terms).astype(BF16)


def shards(members, increment, vertical, spectral_weights, tile_rows):
    levels, stored, columns = increment.shape
    member = members[0]
    table = wave_table(columns)
    basis_x, basis_xt = jnp.asarray(table), jnp.asarray(np.ascontiguousarray(table.T))
    space, mem = lax.axis_index("space"), lax.axis_index("mem")
    z, x, y, core = space // XHI, space % XHI, mem // (XLO * CORE), mem % CORE
    tiles = jnp.stack(
        [(core ^ dc) * Y + (y + dy) % Y for dc in range(CORE) for dy in range(Y)]
    ).astype(jnp.int32)
    rows = tile_rows.shape[0]
    held = tile_rows[None, :]
    chosen = (lax.broadcasted_iota(jnp.int32, (rows, rows), 0) == held).astype(BF16)
    basis_y = jnp.dot(jnp.asarray(wave_table(rows)), chosen, preferred_element_type=F32).astype(BF16)
    basis_yt = basis_y.T
    localized = mix(vertical, member, increment, CHUNKS)
    starts = [sum(CHUNKS[:i]) for i in range(len(CHUNKS))]

    def spread(i):
        return forward(basis_xt, localized[i])

    def damp(pieces):
        return filter_rows(basis_y, basis_yt, spectral_weights, pieces)

    def fold(keep, give):
        return keep, pair_sum(keep, lax.ppermute(give, "mem", mem_to(0, 0, 1)))

    def along_y(keep):
        part = add(
            keep[0], *[lax.ppermute(keep[dy], "mem", mem_to(dy, 0, 0)) for dy in range(1, Y)]
        )
        return add(part, lax.ppermute(part, "mem", mem_to(0, 1, 0)))

    def spread_y(part):
        mine = jnp.stack(
            [part] + [lax.ppermute(part, "mem", mem_to(-dy, 0, 0)) for dy in range(1, Y)]
        )
        return mine, lax.ppermute(mine, "mem", mem_to(0, 0, 1))

    c0 = spread(0)
    r0 = swap(c0)
    c1 = spread(1)
    r1 = swap(c1)
    c2 = spread(2)
    r0, c2 = tie((r0, c2))
    g0 = damp(r0)
    s0 = swap(g0)
    r1, g0, c2 = tie((r1, g0, c2))
    g1 = damp(r1)
    r2 = swap(c2)
    s0, g1 = tie((s0, g1))
    s1 = swap(g1)
    keep0, give0 = backward(tiles, basis_x, member, s0, starts[0])
    keep0, half0 = fold(keep0, give0)
    r2, half0 = tie((r2, half0))
    g2 = damp(r2)
    s2 = swap(g2)
    sum0 = along_y(half0)
    s1, sum0 = tie((s1, sum0))
    keep1, give1 = backward(tiles, basis_x, member, s1, starts[1])
    keep1, half1 = fold(keep1, give1)
    done0 = spread_y(sum0)
    s2, half1, done0 = tie((s2, half1, done0))
    keep2, give2 = backward(tiles, basis_x, member, s2, starts[2])
    keep2, half2 = fold(keep2, give2)
    done1 = spread_y(along_y(half1))
    done2 = spread_y(along_y(half2))
    out = None
    for i, (mine, theirs) in enumerate((done0, done1, done2)):
        out = place(tiles, mine, theirs, out, starts[i], levels)
    return out


def solution(mesh):
    return jax.shard_map(
        shards,
        mesh=mesh,
        in_specs=(
            P("mem", None, "space", None),
            P(None, "space", None),
            P(),
            P(None, "space"),
            P(),
        ),
        out_specs=P(None, "space", None),
        check_vma=False,
    )
```

```python
import math

import jax
import jax.numpy as jnp
import numpy as np
from jax import lax
from jax.experimental import pallas as pl
from jax.experimental.pallas import tpu as pltpu
from jax.sharding import PartitionSpec as P

BF16, F32 = jnp.bfloat16, jnp.float32
LANES = 128
VMEM_LIMIT = 20 * 1024 * 1024
CHUNKS = (46, 46, 45)
STEP = 23


def wave_table(length):
    ranks = np.arange(length)[:, None]
    middle = length // 2
    wavenumber = np.where(ranks <= middle, ranks, ranks - middle)
    angles = wavenumber * np.arange(length)[None, :] % length * (2.0 * math.pi / length)
    edge, inner = 1.0 / math.sqrt(length), math.sqrt(2.0 / length)
    values = np.where(
        ranks == 0,
        edge,
        np.where(
            ranks < middle,
            inner * np.cos(angles),
            np.where(ranks == middle, edge * np.cos(angles), inner * np.sin(angles)),
        ),
    )
    return values.astype(jnp.bfloat16)


def params():
    return pltpu.CompilerParams(vmem_limit_bytes=VMEM_LIMIT)


def mix_kernel(vertical_ref, member_ref, increment_ref, *refs):
    *out_refs, rows, mixed = refs
    levels, stored, _ = member_ref.shape
    tiles = rows.shape[0]
    product = member_ref[...].astype(F32) * increment_ref[...].astype(F32)
    product = product.reshape(levels * stored, tiles * LANES)
    for t in range(tiles):
        rows[t] = product[:, t * LANES : (t + 1) * LANES]
    vertical = vertical_ref[...]
    for p in range(stored):
        at = pl.ds(p, levels, stride=stored)
        block = jnp.concatenate([rows[t, at, :] for t in range(tiles)], axis=1).astype(BF16)
        block = jnp.dot(vertical, block, preferred_element_type=F32)
        for t in range(tiles):
            mixed[t, at, :] = block[:, t * LANES : (t + 1) * LANES]
    start = 0
    for out_ref in out_refs:
        size = out_ref.shape[0]
        for t in range(tiles):
            part = mixed[t, start * stored : (start + size) * stored, :].astype(BF16)
            out_ref[:, :, t * LANES : (t + 1) * LANES] = part.reshape(size, stored, LANES)
        start += size


def mix(vertical, member, increment, chunks, width=256):
    levels, stored, columns = member.shape
    wide = lambda size: pl.BlockSpec((size, stored, width), lambda i: (0, 0, i))
    return pl.pallas_call(
        mix_kernel,
        grid=(columns // width,),
        in_specs=[pl.BlockSpec((levels, levels), lambda i: (0, 0)), wide(levels), wide(levels)],
        out_specs=[wide(size) for size in chunks],
        out_shape=[jax.ShapeDtypeStruct((size, stored, columns), BF16) for size in chunks],
        scratch_shapes=[pltpu.VMEM((width // LANES, levels * stored, LANES), F32)] * 2,
        compiler_params=params(),
        name="mix",
    )(vertical, *[pltpu.with_memory_space_constraint(a, pltpu.HBM) for a in (member, increment)])


def cost(flops, values):
    return pl.CostEstimate(flops=flops, bytes_accessed=2 * values, transcendentals=0)


def at_tile(tile):
    return pl.ds(pl.multiple_of(tile * LANES, LANES), LANES)


def forward_kernel(basis_ref, x_ref, out_ref):
    step, stored, columns = x_ref.shape
    coeffs = jnp.dot(
        x_ref[...].reshape(step * stored, columns), basis_ref[...], preferred_element_type=F32
    ).astype(BF16)
    for d in range(out_ref.shape[0]):
        out_ref[d] = coeffs[:, d * LANES : (d + 1) * LANES].reshape(step, stored, LANES)


def forward(basis, x, at=0):
    size, stored, columns = x.shape
    parts = columns // LANES
    step = min(STEP, size)
    first = at // step
    assert first * step == at
    return pl.pallas_call(
        forward_kernel,
        grid=(pl.cdiv(size, step),),
        in_specs=[
            pl.BlockSpec((columns, columns), lambda i: (0, 0)),
            pl.BlockSpec((step, stored, columns), lambda i: (i, 0, 0)),
        ],
        out_specs=pl.BlockSpec((parts, step, stored, LANES), lambda i: (0, first + i, 0, 0)),
        out_shape=pltpu.HBM((parts, at + size, stored, LANES), BF16),
        compiler_params=params(),
        cost_estimate=cost(2 * x.size * columns, 2 * x.size + basis.size),
        name="forward",
    )(basis, x)


def filter_kernel(basis_ref, basis_t_ref, weights_ref, x_ref, *refs):
    out_ref = refs[-1]
    parts, step, stored, width = x_ref.shape
    x = jnp.concatenate([x_ref[:, l].reshape(parts * stored, width) for l in range(step)], axis=1)
    spectral = jnp.dot(basis_ref[...], x, preferred_element_type=F32)
    weights = jnp.concatenate([weights_ref[...]] * step, axis=1)
    damped = (spectral * weights).astype(BF16)
    back = jnp.dot(basis_t_ref[...], damped, preferred_element_type=F32).astype(BF16)
    for l in range(step):
        out_ref[:, l] = back[:, l * width : (l + 1) * width].reshape(parts, stored, width)


def filter_rows(basis, basis_t, weights, x, start, size, buffer=None):
    parts, _, stored, width = x.shape
    step = min(STEP, size)
    first = start // step
    assert first * step == start
    whole = lambda a: pl.BlockSpec(a.shape, lambda i: (0, 0))
    held = [] if buffer is None else [buffer]
    shape = (parts, size, stored, width) if buffer is None else buffer.shape
    total = parts * size * stored * width
    return pl.pallas_call(
        filter_kernel,
        grid=(pl.cdiv(size, step),),
        in_specs=[whole(basis), whole(basis_t), whole(weights)]
        + [pl.BlockSpec((parts, step, stored, width), lambda i: (0, first + i, 0, 0))]
        + [pl.BlockSpec(memory_space=pl.ANY)] * len(held),
        out_specs=pl.BlockSpec((parts, step, stored, width), lambda i: (0, i, 0, 0)),
        out_shape=pltpu.HBM(shape, BF16),
        input_output_aliases={4: 0} if held else {},
        compiler_params=params(),
        cost_estimate=cost(4 * parts * stored * total, 2 * total),
        name="filter",
    )(basis, basis_t, weights, x, *[pltpu.with_memory_space_constraint(a, pltpu.HBM) for a in held])


def backward_kernel(tiles_ref, basis_ref, member_ref, x_ref, keep_ref, give_ref, held):
    parts, step, stored, width = x_ref.shape
    x = jnp.concatenate([x_ref[d].reshape(step * stored, width) for d in range(parts)], axis=1)
    gridded = jnp.dot(x, basis_ref[...], preferred_element_type=F32)
    held[...] = (member_ref[...].astype(F32).reshape(gridded.shape) * gridded).astype(BF16)
    half = parts // 2
    for q in range(half):
        keep_ref[q] = held[:, at_tile(tiles_ref[q])].reshape(step, stored, width)
        give_ref[q] = held[:, at_tile(tiles_ref[half + q])].reshape(step, stored, width)


def backward(tiles, basis, member, x, start, size):
    parts, _, stored, width = x.shape
    columns = parts * width
    step = min(STEP, size)
    first = start // step
    assert first * step == start
    half = pl.BlockSpec((parts // 2, step, stored, width), lambda i, *_: (0, i, 0, 0))
    total = parts * size * stored * width
    return pl.pallas_call(
        backward_kernel,
        grid_spec=pltpu.PrefetchScalarGridSpec(
            num_scalar_prefetch=1,
            grid=(pl.cdiv(size, step),),
            in_specs=[
                pl.BlockSpec((columns, columns), lambda i, *_: (0, 0)),
                pl.BlockSpec((step, stored, columns), lambda i, *_: (first + i, 0, 0)),
                pl.BlockSpec((parts, step, stored, width), lambda i, *_: (0, i, 0, 0)),
            ],
            out_specs=[half] * 2,
            scratch_shapes=[pltpu.VMEM((step * stored, columns), BF16)],
        ),
        out_shape=[jax.ShapeDtypeStruct((parts // 2, size, stored, width), BF16)] * 2,
        compiler_params=params(),
        cost_estimate=cost(2 * total * columns, 3 * total + basis.size),
        name="backward",
    )(tiles, basis, pltpu.with_memory_space_constraint(member, pltpu.HBM), x)


def pair_kernel(a_ref, b_ref, *out_refs):
    for q, out_ref in enumerate(out_refs):
        out_ref[...] = (a_ref[q].astype(F32) + b_ref[q].astype(F32)).astype(BF16)


def pair_sum(a, b):
    parts, size, stored, width = a.shape
    step = min(STEP, size)
    block = pl.BlockSpec((parts, step, stored, width), lambda i: (0, i, 0, 0))
    return pl.pallas_call(
        pair_kernel,
        grid=(pl.cdiv(size, step),),
        in_specs=[block] * 2,
        out_specs=[pl.BlockSpec((step, stored, width), lambda i: (i, 0, 0))] * parts,
        out_shape=[jax.ShapeDtypeStruct(a.shape[1:], BF16)] * parts,
        compiler_params=params(),
        cost_estimate=cost(a.size, 3 * a.size),
        name="pair_sum",
    )(a, b)


def place_kernel(tiles_ref, mine_ref, theirs_ref, *refs):
    out_ref = refs[-1]
    half = mine_ref.shape[0]
    for q in range(half):
        out_ref[:, :, at_tile(tiles_ref[q])] = mine_ref[q]
        out_ref[:, :, at_tile(tiles_ref[half + q])] = theirs_ref[q]


def place(tiles, mine, theirs, out, start, levels):
    half, size, stored, width = mine.shape
    columns = 2 * half * width
    step = min(STEP, size)
    first = start // step
    block = pl.BlockSpec((half, step, stored, width), lambda i, *_: (0, i, 0, 0))
    held = [] if out is None else [out]
    return pl.pallas_call(
        place_kernel,
        grid_spec=pltpu.PrefetchScalarGridSpec(
            num_scalar_prefetch=1,
            grid=(pl.cdiv(size, step),),
            in_specs=[block] * 2 + [pl.BlockSpec(memory_space=pl.ANY)] * len(held),
            out_specs=pl.BlockSpec((step, stored, columns), lambda i, *_: (first + i, 0, 0)),
        ),
        out_shape=jax.ShapeDtypeStruct((levels, stored, columns), BF16),
        input_output_aliases={3: 0} if held else {},
        compiler_params=params(),
        cost_estimate=cost(0, 4 * mine.size),
        name="place",
    )(tiles, mine, theirs, *held)


Y, XLO, CORE, Z, XHI = 4, 2, 2, 4, 2


def space_to(dz, dx):
    return [(z * XHI + x, (z + dz) % Z * XHI + (x ^ dx)) for z in range(Z) for x in range(XHI)]


def mem_to(dy, dx, dc):
    return [
        ((y * XLO + x) * CORE + c, ((y + dy) % Y * XLO + (x ^ dx)) * CORE + (c ^ dc))
        for y in range(Y)
        for x in range(XLO)
        for c in range(CORE)
    ]


def swap(pieces):
    return lax.all_to_all(pieces, "space", 0, 0, tiled=True)


tie = lax.optimization_barrier


def add(*terms):
    return sum(t.astype(F32) for t in terms).astype(BF16)


def shards(members, increment, vertical, spectral_weights, tile_rows):
    levels, stored, columns = increment.shape
    member = members[0]
    table = wave_table(columns)
    basis_x, basis_xt = jnp.asarray(table), jnp.asarray(np.ascontiguousarray(table.T))
    space, mem = lax.axis_index("space"), lax.axis_index("mem")
    z, x, y, core = space // XHI, space % XHI, mem // (XLO * CORE), mem % CORE
    tiles = jnp.stack(
        [(core ^ dc) * Y + (y + dy) % Y for dc in range(CORE) for dy in range(Y)]
    ).astype(jnp.int32)
    rows = tile_rows.shape[0]
    held = tile_rows[None, :]
    chosen = (lax.broadcasted_iota(jnp.int32, (rows, rows), 0) == held).astype(BF16)
    basis_y = jnp.dot(jnp.asarray(wave_table(rows)), chosen, preferred_element_type=F32).astype(BF16)
    basis_yt = basis_y.T
    localized = mix(vertical, member, increment, CHUNKS)
    starts = [sum(CHUNKS[:i]) for i in range(len(CHUNKS))]

    def spread(i):
        return forward(basis_xt, localized[i], CHUNKS[i - 1] if i else 0)

    def damp(i, came, buffer=None):
        start = CHUNKS[i - 1] if i else 0
        return filter_rows(basis_y, basis_yt, spectral_weights, came, start, CHUNKS[i], buffer)

    def regrid(i, came):
        return backward(tiles, basis_x, member, came, starts[i], CHUNKS[i])

    def fold(keep, give):
        return pair_sum(keep, lax.ppermute(give, "mem", mem_to(0, 0, 1)))

    def scatter(kept):
        return [kept[0]] + [lax.ppermute(kept[dy], "mem", mem_to(dy, 0, 0)) for dy in range(1, Y)]

    def cross(part):
        return lax.ppermute(part, "mem", mem_to(0, 1, 0))

    def collect(part):
        return [part] + [lax.ppermute(part, "mem", mem_to(-dy, 0, 0)) for dy in range(1, Y)]

    def give(parts):
        mine = jnp.stack(parts)
        return mine, lax.ppermute(mine, "mem", mem_to(0, 0, 1))

    def along_y(keep):
        part = add(*scatter(keep))
        return add(part, cross(part))

    came = swap(spread(0))
    buffer = spread(1)
    came, buffer = tie((came, buffer))
    came = swap(damp(0, came, buffer))
    buffer = spread(2)
    came, buffer = tie((came, buffer))
    next_came = swap(damp(1, came, buffer))
    half0 = fold(*regrid(0, came))
    sum0 = along_y(half0)
    came, sum0 = tie((next_came, sum0))
    last = swap(damp(2, came))
    half1 = fold(*regrid(1, came))
    done0 = give(collect(sum0))
    last, half1, done0 = tie((last, half1, done0))
    half2 = fold(*regrid(2, last))
    done1 = give(collect(along_y(half1)))
    done2 = give(collect(along_y(half2)))
    out = None
    for i, (mine, theirs) in enumerate((done0, done1, done2)):
        out = place(tiles, mine, theirs, out, starts[i], levels)
    return out


def solution(mesh):
    return jax.shard_map(
        shards,
        mesh=mesh,
        in_specs=(
            P("mem", None, "space", None),
            P(None, "space", None),
            P(),
            P(None, "space"),
            P(),
        ),
        out_specs=P(None, "space", None),
        check_vma=False,
    )
```

```python
import math

import jax
import jax.numpy as jnp
import numpy as np
from jax import lax
from jax.experimental import pallas as pl
from jax.experimental.pallas import tpu as pltpu
from jax.sharding import PartitionSpec as P

BF16, F32 = jnp.bfloat16, jnp.float32
LANES = 128
VMEM_LIMIT = 20 * 1024 * 1024
CHUNKS = (46, 46, 45)
STEP = 23
SHORT = 23


def wave_table(length):
    ranks = np.arange(length)[:, None]
    middle = length // 2
    wavenumber = np.where(ranks <= middle, ranks, ranks - middle)
    angles = wavenumber * np.arange(length)[None, :] % length * (2.0 * math.pi / length)
    edge, inner = 1.0 / math.sqrt(length), math.sqrt(2.0 / length)
    values = np.where(
        ranks == 0,
        edge,
        np.where(
            ranks < middle,
            inner * np.cos(angles),
            np.where(ranks == middle, edge * np.cos(angles), inner * np.sin(angles)),
        ),
    )
    return values.astype(jnp.bfloat16)


def params():
    return pltpu.CompilerParams(vmem_limit_bytes=VMEM_LIMIT)


def mix_kernel(vertical_ref, basis_ref, member_ref, increment_ref, coeffs_ref, *refs):
    *out_refs, total = refs
    vertical = vertical_ref[...]
    product = jnp.swapaxes(member_ref[...] * increment_ref[...], 0, 1)
    mixed = [
        jnp.dot(vertical, product[p], preferred_element_type=F32).astype(BF16)
        for p in range(product.shape[0])
    ]
    mixed = jnp.swapaxes(jnp.stack(mixed, axis=0), 0, 1)
    parts, start, stored, _ = coeffs_ref.shape
    first = mixed[:start].reshape(start * stored, mixed.shape[-1])
    more = jnp.dot(first, basis_ref[...], preferred_element_type=F32)
    step, last = pl.program_id(0), pl.num_programs(0) - 1

    @pl.when(step == 0)
    def _():
        total[...] = more

    @pl.when((step > 0) & (step < last))
    def _():
        total[...] += more

    @pl.when(step == last)
    def _():
        done = (total[...] + more).astype(BF16)
        for s in range(parts):
            coeffs_ref[s] = done[:, s * LANES : (s + 1) * LANES].reshape(start, stored, LANES)

    for out_ref in out_refs:
        size = out_ref.shape[0]
        out_ref[...] = mixed[start : start + size]
        start += size


def mix(vertical, basis, member, increment, chunks, width=256):
    levels, stored, columns = member.shape
    parts = columns // LANES
    wide = lambda size: pl.BlockSpec((size, stored, width), lambda i: (0, 0, i))
    first = (parts, chunks[0], stored, LANES)
    return pl.pallas_call(
        mix_kernel,
        grid=(columns // width,),
        in_specs=[
            pl.BlockSpec((levels, levels), lambda i: (0, 0)),
            pl.BlockSpec((width, columns), lambda i: (i, 0)),
            wide(levels),
            wide(levels),
        ],
        out_specs=[pl.BlockSpec(first, lambda i: (0, 0, 0, 0))] + [wide(n) for n in chunks[1:]],
        out_shape=[pltpu.HBM(first, BF16)]
        + [pltpu.HBM((n, stored, columns), BF16) for n in chunks[1:]],
        scratch_shapes=[pltpu.VMEM((chunks[0] * stored, columns), F32)],
        compiler_params=pltpu.CompilerParams(vmem_limit_bytes=40 * 1024 * 1024),
        name="mix",
    )(vertical, *[pltpu.with_memory_space_constraint(a, pltpu.HBM) for a in (basis, member, increment)])


def cost(flops, values):
    return pl.CostEstimate(flops=flops, bytes_accessed=2 * values, transcendentals=0)


def at_tile(tile):
    return pl.ds(pl.multiple_of(tile * LANES, LANES), LANES)


def forward_kernel(basis_ref, x_ref, out_ref):
    step, stored, columns = x_ref.shape
    coeffs = jnp.dot(
        x_ref[...].reshape(step * stored, columns), basis_ref[...], preferred_element_type=F32
    ).astype(BF16)
    for d in range(out_ref.shape[0]):
        out_ref[d] = coeffs[:, d * LANES : (d + 1) * LANES].reshape(step, stored, LANES)


def forward(basis, x, at=0):
    size, stored, columns = x.shape
    parts = columns // LANES
    step = min(STEP, size)
    first = at // step
    assert first * step == at
    return pl.pallas_call(
        forward_kernel,
        grid=(pl.cdiv(size, step),),
        in_specs=[
            pl.BlockSpec((columns, columns), lambda i: (0, 0)),
            pl.BlockSpec((step, stored, columns), lambda i: (i, 0, 0)),
        ],
        out_specs=pl.BlockSpec((parts, step, stored, LANES), lambda i: (0, first + i, 0, 0)),
        out_shape=pltpu.HBM((parts, at + size, stored, LANES), BF16),
        compiler_params=params(),
        cost_estimate=cost(2 * x.size * columns, 2 * x.size + basis.size),
        name="forward",
    )(basis, pltpu.with_memory_space_constraint(x, pltpu.HBM))


def filter_kernel(basis_ref, basis_t_ref, weights_ref, x_ref, *refs):
    out_ref = refs[-1]
    parts, step, stored, width = x_ref.shape
    x = jnp.concatenate([x_ref[:, l].reshape(parts * stored, width) for l in range(step)], axis=1)
    spectral = jnp.dot(basis_ref[...], x, preferred_element_type=F32)
    weights = jnp.concatenate([weights_ref[...]] * step, axis=1)
    damped = (spectral * weights).astype(BF16)
    back = jnp.dot(basis_t_ref[...], damped, preferred_element_type=F32).astype(BF16)
    for l in range(step):
        out_ref[:, l] = back[:, l * width : (l + 1) * width].reshape(parts, stored, width)


def filter_rows(basis, basis_t, weights, x, start, size, buffer=None):
    parts, _, stored, width = x.shape
    step = min(SHORT, size)
    first = start // step
    assert first * step == start
    whole = lambda a: pl.BlockSpec(a.shape, lambda i: (0, 0))
    held = [] if buffer is None else [buffer]
    shape = (parts, size, stored, width) if buffer is None else buffer.shape
    total = parts * size * stored * width
    return pl.pallas_call(
        filter_kernel,
        grid=(pl.cdiv(size, step),),
        in_specs=[whole(basis), whole(basis_t), whole(weights)]
        + [pl.BlockSpec((parts, step, stored, width), lambda i: (0, first + i, 0, 0))]
        + [pl.BlockSpec(memory_space=pl.ANY)] * len(held),
        out_specs=pl.BlockSpec((parts, step, stored, width), lambda i: (0, i, 0, 0)),
        out_shape=pltpu.HBM(shape, BF16),
        input_output_aliases={4: 0} if held else {},
        compiler_params=params(),
        cost_estimate=cost(4 * parts * stored * total, 2 * total),
        name="filter",
    )(basis, basis_t, weights, x, *[pltpu.with_memory_space_constraint(a, pltpu.HBM) for a in held])


def backward_kernel(tiles_ref, basis_ref, member_ref, x_ref, keep_ref, give_ref, held):
    parts, step, stored, width = x_ref.shape
    x = jnp.concatenate([x_ref[d].reshape(step * stored, width) for d in range(parts)], axis=1)
    gridded = jnp.dot(x, basis_ref[...], preferred_element_type=F32)
    held[...] = (member_ref[...].astype(F32).reshape(gridded.shape) * gridded).astype(BF16)
    half = parts // 2
    for q in range(half):
        keep_ref[q] = held[:, at_tile(tiles_ref[q])].reshape(step, stored, width)
        give_ref[q] = held[:, at_tile(tiles_ref[half + q])].reshape(step, stored, width)


def backward(tiles, basis, member, x, start, size):
    parts, _, stored, width = x.shape
    columns = parts * width
    step = min(STEP, size)
    first = start // step
    assert first * step == start
    half = pl.BlockSpec((parts // 2, step, stored, width), lambda i, *_: (0, i, 0, 0))
    total = parts * size * stored * width
    return pl.pallas_call(
        backward_kernel,
        grid_spec=pltpu.PrefetchScalarGridSpec(
            num_scalar_prefetch=1,
            grid=(pl.cdiv(size, step),),
            in_specs=[
                pl.BlockSpec((columns, columns), lambda i, *_: (0, 0)),
                pl.BlockSpec((step, stored, columns), lambda i, *_: (first + i, 0, 0)),
                pl.BlockSpec((parts, step, stored, width), lambda i, *_: (0, i, 0, 0)),
            ],
            out_specs=[half] * 2,
            scratch_shapes=[pltpu.VMEM((step * stored, columns), BF16)],
        ),
        out_shape=[jax.ShapeDtypeStruct((parts // 2, size, stored, width), BF16)] * 2,
        compiler_params=params(),
        cost_estimate=cost(2 * total * columns, 3 * total + basis.size),
        name="backward",
    )(tiles, basis, pltpu.with_memory_space_constraint(member, pltpu.HBM), x)


def pair_kernel(a_ref, b_ref, *out_refs):
    for q, out_ref in enumerate(out_refs):
        out_ref[...] = (a_ref[q].astype(F32) + b_ref[q].astype(F32)).astype(BF16)


def pair_sum(a, b):
    parts, size, stored, width = a.shape
    step = min(STEP, size)
    block = pl.BlockSpec((parts, step, stored, width), lambda i: (0, i, 0, 0))
    return pl.pallas_call(
        pair_kernel,
        grid=(pl.cdiv(size, step),),
        in_specs=[block] * 2,
        out_specs=[pl.BlockSpec((step, stored, width), lambda i: (i, 0, 0))] * parts,
        out_shape=[jax.ShapeDtypeStruct(a.shape[1:], BF16)] * parts,
        compiler_params=params(),
        cost_estimate=cost(a.size, 3 * a.size),
        name="pair_sum",
    )(a, b)


def place_kernel(tiles_ref, mine_ref, theirs_ref, *refs):
    out_ref = refs[-1]
    half = mine_ref.shape[0]
    for q in range(half):
        out_ref[:, :, at_tile(tiles_ref[q])] = mine_ref[q]
        out_ref[:, :, at_tile(tiles_ref[half + q])] = theirs_ref[q]


def place(tiles, mine, theirs, out, start, levels):
    half, size, stored, width = mine.shape
    columns = 2 * half * width
    step = min(STEP, size)
    first = start // step
    block = pl.BlockSpec((half, step, stored, width), lambda i, *_: (0, i, 0, 0))
    held = [] if out is None else [out]
    return pl.pallas_call(
        place_kernel,
        grid_spec=pltpu.PrefetchScalarGridSpec(
            num_scalar_prefetch=1,
            grid=(pl.cdiv(size, step),),
            in_specs=[block] * 2 + [pl.BlockSpec(memory_space=pl.ANY)] * len(held),
            out_specs=pl.BlockSpec((step, stored, columns), lambda i, *_: (first + i, 0, 0)),
        ),
        out_shape=jax.ShapeDtypeStruct((levels, stored, columns), BF16),
        input_output_aliases={3: 0} if held else {},
        compiler_params=params(),
        cost_estimate=cost(0, 4 * mine.size),
        name="place",
    )(tiles, mine, theirs, *held)


Y, XLO, CORE, Z, XHI = 4, 2, 2, 4, 2


def space_to(dz, dx):
    return [(z * XHI + x, (z + dz) % Z * XHI + (x ^ dx)) for z in range(Z) for x in range(XHI)]


def mem_to(dy, dx, dc):
    return [
        ((y * XLO + x) * CORE + c, ((y + dy) % Y * XLO + (x ^ dx)) * CORE + (c ^ dc))
        for y in range(Y)
        for x in range(XLO)
        for c in range(CORE)
    ]


def swap(pieces):
    return lax.all_to_all(pieces, "space", 0, 0, tiled=True)


tie = lax.optimization_barrier


def add(*terms):
    return sum(t.astype(F32) for t in terms).astype(BF16)


def shards(members, increment, vertical, spectral_weights, tile_rows):
    levels, stored, columns = increment.shape
    member = members[0]
    table = wave_table(columns)
    basis_x, basis_xt = jnp.asarray(table), jnp.asarray(np.ascontiguousarray(table.T))
    space, mem = lax.axis_index("space"), lax.axis_index("mem")
    z, x, y, core = space // XHI, space % XHI, mem // (XLO * CORE), mem % CORE
    tiles = jnp.stack(
        [(core ^ dc) * Y + (y + dy) % Y for dc in range(CORE) for dy in range(Y)]
    ).astype(jnp.int32)
    rows = tile_rows.shape[0]
    held = tile_rows[None, :]
    chosen = (lax.broadcasted_iota(jnp.int32, (rows, rows), 0) == held).astype(BF16)
    basis_y = jnp.dot(jnp.asarray(wave_table(rows)), chosen, preferred_element_type=F32).astype(BF16)
    basis_yt = basis_y.T
    localized = mix(vertical, basis_xt, member, increment, CHUNKS)
    starts = [sum(CHUNKS[:i]) for i in range(len(CHUNKS))]

    def spread(i):
        return forward(basis_xt, localized[i], CHUNKS[i - 1])

    def damp(i, came, buffer=None):
        start = CHUNKS[i - 1] if i else 0
        return filter_rows(basis_y, basis_yt, spectral_weights, came, start, CHUNKS[i], buffer)

    def regrid(i, came):
        return backward(tiles, basis_x, member, came, starts[i], CHUNKS[i])

    def fold(keep, give):
        return pair_sum(keep, lax.ppermute(give, "mem", mem_to(0, 0, 1)))

    def scatter(kept):
        return [kept[0]] + [lax.ppermute(kept[dy], "mem", mem_to(dy, 0, 0)) for dy in range(1, Y)]

    def cross(part):
        return lax.ppermute(part, "mem", mem_to(0, 1, 0))

    def collect(part):
        return [part] + [lax.ppermute(part, "mem", mem_to(-dy, 0, 0)) for dy in range(1, Y)]

    def give(parts):
        mine = jnp.stack(parts)
        return mine, lax.ppermute(mine, "mem", mem_to(0, 0, 1))

    def along_y(keep):
        part = add(*scatter(keep))
        return add(part, cross(part))

    came = swap(localized[0])
    buffer = spread(1)
    came, buffer = tie((came, buffer))
    came = swap(damp(0, came, buffer))
    buffer = spread(2)
    came, buffer = tie((came, buffer))
    next_came = swap(damp(1, came, buffer))
    half0 = fold(*regrid(0, came))
    sum0 = along_y(half0)
    came, sum0 = tie((next_came, sum0))
    last = swap(damp(2, came))
    half1 = fold(*regrid(1, came))
    done0 = give(collect(sum0))
    last, half1, done0 = tie((last, half1, done0))
    half2 = fold(*regrid(2, last))
    done1 = give(collect(along_y(half1)))
    done2 = give(collect(along_y(half2)))
    out = None
    for i, (mine, theirs) in enumerate((done0, done1, done2)):
        out = place(tiles, mine, theirs, out, starts[i], levels)
    return out


def solution(mesh):
    return jax.shard_map(
        shards,
        mesh=mesh,
        in_specs=(
            P("mem", None, "space", None),
            P(None, "space", None),
            P(),
            P(None, "space"),
            P(),
        ),
        out_specs=P(None, "space", None),
        check_vma=False,
    )
```

```python
import math

import jax
import jax.numpy as jnp
import numpy as np
from jax import lax
from jax.experimental import pallas as pl
from jax.experimental.pallas import tpu as pltpu
from jax.sharding import PartitionSpec as P

BF16, F32 = jnp.bfloat16, jnp.float32
LANES = 128
VMEM_LIMIT = 30 * 1024 * 1024
CHUNKS = (46, 46, 45)
STEP = 23
SHORT = 23


def wave_table(length):
    ranks = np.arange(length)[:, None]
    middle = length // 2
    wavenumber = np.where(ranks <= middle, ranks, ranks - middle)
    angles = wavenumber * np.arange(length)[None, :] % length * (2.0 * math.pi / length)
    edge, inner = 1.0 / math.sqrt(length), math.sqrt(2.0 / length)
    values = np.where(
        ranks == 0,
        edge,
        np.where(
            ranks < middle,
            inner * np.cos(angles),
            np.where(ranks == middle, edge * np.cos(angles), inner * np.sin(angles)),
        ),
    )
    return values.astype(jnp.bfloat16)


def params():
    return pltpu.CompilerParams(vmem_limit_bytes=VMEM_LIMIT)


def mix_kernel(vertical_ref, basis_ref, member_ref, increment_ref, coeffs_ref, *refs):
    *out_refs, total = refs
    vertical = vertical_ref[...]
    product = jnp.swapaxes(member_ref[...] * increment_ref[...], 0, 1)
    mixed = [
        jnp.dot(vertical, product[p], preferred_element_type=F32).astype(BF16)
        for p in range(product.shape[0])
    ]
    mixed = jnp.swapaxes(jnp.stack(mixed, axis=0), 0, 1)
    parts, start, stored, _ = coeffs_ref.shape
    first = mixed[:start].reshape(start * stored, mixed.shape[-1])
    more = jnp.dot(first, basis_ref[...], preferred_element_type=F32)
    step, last = pl.program_id(0), pl.num_programs(0) - 1

    @pl.when(step == 0)
    def _():
        total[...] = more

    @pl.when((step > 0) & (step < last))
    def _():
        total[...] += more

    @pl.when(step == last)
    def _():
        done = (total[...] + more).astype(BF16)
        for s in range(parts):
            coeffs_ref[s] = done[:, s * LANES : (s + 1) * LANES].reshape(start, stored, LANES)

    for out_ref in out_refs:
        size = out_ref.shape[0]
        out_ref[...] = mixed[start : start + size]
        start += size


def mix(vertical, basis, member, increment, chunks, width=256):
    levels, stored, columns = member.shape
    parts = columns // LANES
    wide = lambda size: pl.BlockSpec((size, stored, width), lambda i: (0, 0, i))
    first = (parts, chunks[0], stored, LANES)
    return pl.pallas_call(
        mix_kernel,
        grid=(columns // width,),
        in_specs=[
            pl.BlockSpec((levels, levels), lambda i: (0, 0)),
            pl.BlockSpec((width, columns), lambda i: (i, 0)),
            wide(levels),
            wide(levels),
        ],
        out_specs=[pl.BlockSpec(first, lambda i: (0, 0, 0, 0))] + [wide(n) for n in chunks[1:]],
        out_shape=[pltpu.HBM(first, BF16)]
        + [pltpu.HBM((n, stored, columns), BF16) for n in chunks[1:]],
        scratch_shapes=[pltpu.VMEM((chunks[0] * stored, columns), F32)],
        compiler_params=pltpu.CompilerParams(vmem_limit_bytes=40 * 1024 * 1024),
        name="mix",
    )(vertical, *[pltpu.with_memory_space_constraint(a, pltpu.HBM) for a in (basis, member, increment)])


def cost(flops, values):
    return pl.CostEstimate(flops=flops, bytes_accessed=2 * values, transcendentals=0)


def at_tile(tile):
    return pl.ds(pl.multiple_of(tile * LANES, LANES), LANES)


def forward_kernel(basis_ref, x_ref, out_ref):
    step, stored, columns = x_ref.shape
    coeffs = jnp.dot(
        x_ref[...].reshape(step * stored, columns), basis_ref[...], preferred_element_type=F32
    ).astype(BF16)
    for d in range(out_ref.shape[0]):
        out_ref[d] = coeffs[:, d * LANES : (d + 1) * LANES].reshape(step, stored, LANES)


def forward(basis, x, at=0):
    size, stored, columns = x.shape
    parts = columns // LANES
    step = min(STEP, size)
    first = at // step
    assert first * step == at
    return pl.pallas_call(
        forward_kernel,
        grid=(pl.cdiv(size, step),),
        in_specs=[
            pl.BlockSpec((columns, columns), lambda i: (0, 0)),
            pl.BlockSpec((step, stored, columns), lambda i: (i, 0, 0)),
        ],
        out_specs=pl.BlockSpec((parts, step, stored, LANES), lambda i: (0, first + i, 0, 0)),
        out_shape=pltpu.HBM((parts, at + size, stored, LANES), BF16),
        compiler_params=params(),
        cost_estimate=cost(2 * x.size * columns, 2 * x.size + basis.size),
        name="forward",
    )(basis, pltpu.with_memory_space_constraint(x, pltpu.HBM))


def filter_kernel(basis_ref, basis_t_ref, weights_ref, x_ref, *refs):
    out_ref = refs[-1]
    parts, step, stored, width = x_ref.shape
    x = jnp.concatenate([x_ref[:, l].reshape(parts * stored, width) for l in range(step)], axis=1)
    spectral = jnp.dot(basis_ref[...], x, preferred_element_type=F32)
    weights = jnp.concatenate([weights_ref[...]] * step, axis=1)
    damped = (spectral * weights).astype(BF16)
    back = jnp.dot(basis_t_ref[...], damped, preferred_element_type=F32).astype(BF16)
    for l in range(step):
        out_ref[:, l] = back[:, l * width : (l + 1) * width].reshape(parts, stored, width)


def filter_rows(basis, basis_t, weights, x, start, size, buffer=None):
    parts, _, stored, width = x.shape
    step = min(SHORT, size)
    first = start // step
    assert first * step == start
    whole = lambda a: pl.BlockSpec(a.shape, lambda i: (0, 0))
    held = [] if buffer is None else [buffer]
    shape = (parts, size, stored, width) if buffer is None else buffer.shape
    total = parts * size * stored * width
    return pl.pallas_call(
        filter_kernel,
        grid=(pl.cdiv(size, step),),
        in_specs=[whole(basis), whole(basis_t), whole(weights)]
        + [pl.BlockSpec((parts, step, stored, width), lambda i: (0, first + i, 0, 0))]
        + [pl.BlockSpec(memory_space=pl.ANY)] * len(held),
        out_specs=pl.BlockSpec((parts, step, stored, width), lambda i: (0, i, 0, 0)),
        out_shape=pltpu.HBM(shape, BF16),
        input_output_aliases={4: 0} if held else {},
        compiler_params=params(),
        cost_estimate=cost(4 * parts * stored * total, 2 * total),
        name="filter",
    )(basis, basis_t, weights, x, *[pltpu.with_memory_space_constraint(a, pltpu.HBM) for a in held])


def backward_kernel(tiles_ref, basis_ref, member_ref, x_ref, keep_ref, give_ref, held):
    parts, step, stored, width = x_ref.shape
    x = jnp.concatenate([x_ref[d].reshape(step * stored, width) for d in range(parts)], axis=1)
    gridded = jnp.dot(x, basis_ref[...], preferred_element_type=F32)
    held[...] = (member_ref[...].astype(F32).reshape(gridded.shape) * gridded).astype(BF16)
    half = parts // 2
    for q in range(half):
        keep_ref[q] = held[:, at_tile(tiles_ref[q])].reshape(step, stored, width)
        give_ref[q] = held[:, at_tile(tiles_ref[half + q])].reshape(step, stored, width)


def backward(tiles, basis, member, x, start, size):
    parts, _, stored, width = x.shape
    columns = parts * width
    step = min(STEP, size)
    first = start // step
    assert first * step == start
    half = pl.BlockSpec((parts // 2, step, stored, width), lambda i, *_: (0, i, 0, 0))
    total = parts * size * stored * width
    return pl.pallas_call(
        backward_kernel,
        grid_spec=pltpu.PrefetchScalarGridSpec(
            num_scalar_prefetch=1,
            grid=(pl.cdiv(size, step),),
            in_specs=[
                pl.BlockSpec((columns, columns), lambda i, *_: (0, 0)),
                pl.BlockSpec((step, stored, columns), lambda i, *_: (first + i, 0, 0)),
                pl.BlockSpec((parts, step, stored, width), lambda i, *_: (0, i, 0, 0)),
            ],
            out_specs=[half] * 2,
            scratch_shapes=[pltpu.VMEM((step * stored, columns), BF16)],
        ),
        out_shape=[jax.ShapeDtypeStruct((parts // 2, size, stored, width), BF16)] * 2,
        compiler_params=params(),
        cost_estimate=cost(2 * total * columns, 3 * total + basis.size),
        name="backward",
    )(tiles, basis, pltpu.with_memory_space_constraint(member, pltpu.HBM), x)


def pair_kernel(a_ref, b_ref, *out_refs):
    for q, out_ref in enumerate(out_refs):
        out_ref[...] = (a_ref[q].astype(F32) + b_ref[q].astype(F32)).astype(BF16)


def pair_sum(a, b):
    parts, size, stored, width = a.shape
    step = min(STEP, size)
    block = pl.BlockSpec((parts, step, stored, width), lambda i: (0, i, 0, 0))
    return pl.pallas_call(
        pair_kernel,
        grid=(pl.cdiv(size, step),),
        in_specs=[block] * 2,
        out_specs=[pl.BlockSpec((step, stored, width), lambda i: (i, 0, 0))] * parts,
        out_shape=[jax.ShapeDtypeStruct(a.shape[1:], BF16)] * parts,
        compiler_params=params(),
        cost_estimate=cost(a.size, 3 * a.size),
        name="pair_sum",
    )(a, b)


def place_kernel(tiles_ref, mine_ref, theirs_ref, *refs):
    out_ref = refs[-1]
    half = mine_ref.shape[0]
    for q in range(half):
        out_ref[:, :, at_tile(tiles_ref[q])] = mine_ref[q]
        out_ref[:, :, at_tile(tiles_ref[half + q])] = theirs_ref[q]


def place(tiles, mine, theirs, out, start, levels):
    half, size, stored, width = mine.shape
    columns = 2 * half * width
    step = min(STEP, size)
    first = start // step
    block = pl.BlockSpec((half, step, stored, width), lambda i, *_: (0, i, 0, 0))
    held = [] if out is None else [out]
    return pl.pallas_call(
        place_kernel,
        grid_spec=pltpu.PrefetchScalarGridSpec(
            num_scalar_prefetch=1,
            grid=(pl.cdiv(size, step),),
            in_specs=[block] * 2 + [pl.BlockSpec(memory_space=pl.ANY)] * len(held),
            out_specs=pl.BlockSpec((step, stored, columns), lambda i, *_: (first + i, 0, 0)),
        ),
        out_shape=jax.ShapeDtypeStruct((levels, stored, columns), BF16),
        input_output_aliases={3: 0} if held else {},
        compiler_params=params(),
        cost_estimate=cost(0, 4 * mine.size),
        name="place",
    )(tiles, mine, theirs, *held)


Y, XLO, CORE, Z, XHI = 4, 2, 2, 4, 2


def space_to(dz, dx):
    return [(z * XHI + x, (z + dz) % Z * XHI + (x ^ dx)) for z in range(Z) for x in range(XHI)]


def mem_to(dy, dx, dc):
    return [
        ((y * XLO + x) * CORE + c, ((y + dy) % Y * XLO + (x ^ dx)) * CORE + (c ^ dc))
        for y in range(Y)
        for x in range(XLO)
        for c in range(CORE)
    ]


def swap(pieces):
    return lax.all_to_all(pieces, "space", 0, 0, tiled=True)


tie = lax.optimization_barrier


def add(*terms):
    return sum(t.astype(F32) for t in terms).astype(BF16)


def shards(members, increment, vertical, spectral_weights, tile_rows):
    levels, stored, columns = increment.shape
    member = members[0]
    table = wave_table(columns)
    basis_x, basis_xt = jnp.asarray(table), jnp.asarray(np.ascontiguousarray(table.T))
    space, mem = lax.axis_index("space"), lax.axis_index("mem")
    z, x, y, core = space // XHI, space % XHI, mem // (XLO * CORE), mem % CORE
    tiles = jnp.stack(
        [(core ^ dc) * Y + (y + dy) % Y for dc in range(CORE) for dy in range(Y)]
    ).astype(jnp.int32)
    rows = tile_rows.shape[0]
    held = tile_rows[None, :]
    chosen = (lax.broadcasted_iota(jnp.int32, (rows, rows), 0) == held).astype(BF16)
    basis_y = jnp.dot(jnp.asarray(wave_table(rows)), chosen, preferred_element_type=F32).astype(BF16)
    basis_yt = basis_y.T
    localized = mix(vertical, basis_xt, member, increment, CHUNKS)
    starts = [sum(CHUNKS[:i]) for i in range(len(CHUNKS))]

    def spread(i):
        return forward(basis_xt, localized[i], CHUNKS[i - 1])

    def damp(i, came, buffer=None):
        start = CHUNKS[i - 1] if i else 0
        return filter_rows(basis_y, basis_yt, spectral_weights, came, start, CHUNKS[i], buffer)

    def regrid(i, came):
        return backward(tiles, basis_x, member, came, starts[i], CHUNKS[i])

    def fold(keep, give):
        return pair_sum(keep, lax.ppermute(give, "mem", mem_to(0, 0, 1)))

    def scatter(kept):
        return [kept[0]] + [lax.ppermute(kept[dy], "mem", mem_to(dy, 0, 0)) for dy in range(1, Y)]

    def cross(part):
        return lax.ppermute(part, "mem", mem_to(0, 1, 0))

    def collect(part):
        return [part] + [lax.ppermute(part, "mem", mem_to(-dy, 0, 0)) for dy in range(1, Y)]

    def give(parts):
        mine = jnp.stack(parts)
        return mine, lax.ppermute(mine, "mem", mem_to(0, 0, 1))

    def along_y(keep):
        part = add(*scatter(keep))
        return add(part, cross(part))

    came = swap(localized[0])
    buffer = spread(1)
    came, buffer = tie((came, buffer))
    came = swap(damp(0, came, buffer))
    buffer = spread(2)
    came, buffer = tie((came, buffer))
    next_came = swap(damp(1, came, buffer))
    half0 = fold(*regrid(0, came))
    sum0 = along_y(half0)
    came, sum0 = tie((next_came, sum0))
    last = swap(damp(2, came))
    half1 = fold(*regrid(1, came))
    done0 = give(collect(sum0))
    last, half1, done0 = tie((last, half1, done0))
    half2 = fold(*regrid(2, last))
    done1 = give(collect(along_y(half1)))
    done2 = collect(along_y(half2))
    out = place(tiles, *done0, None, starts[0], levels)
    done2, out = tie((done2, out))
    out = place(tiles, *done1, out, starts[1], levels)
    return place(tiles, *give(done2), out, starts[2], levels)


def solution(mesh):
    return jax.shard_map(
        shards,
        mesh=mesh,
        in_specs=(
            P("mem", None, "space", None),
            P(None, "space", None),
            P(),
            P(None, "space"),
            P(),
        ),
        out_specs=P(None, "space", None),
        check_vma=False,
    )
```

```python
import math

import jax
import jax.numpy as jnp
import numpy as np
from jax import lax
from jax.experimental import pallas as pl
from jax.experimental.pallas import tpu as pltpu
from jax.sharding import PartitionSpec as P

BF16, F32 = jnp.bfloat16, jnp.float32
LANES = 128
VMEM_LIMIT = 30 * 1024 * 1024
CHUNKS = (46, 46, 45)
STEP = 23
SHORT = 23


def wave_table(length):
    ranks = np.arange(length)[:, None]
    middle = length // 2
    wavenumber = np.where(ranks <= middle, ranks, ranks - middle)
    angles = wavenumber * np.arange(length)[None, :] % length * (2.0 * math.pi / length)
    edge, inner = 1.0 / math.sqrt(length), math.sqrt(2.0 / length)
    values = np.where(
        ranks == 0,
        edge,
        np.where(
            ranks < middle,
            inner * np.cos(angles),
            np.where(ranks == middle, edge * np.cos(angles), inner * np.sin(angles)),
        ),
    )
    return values.astype(jnp.bfloat16)


def params():
    return pltpu.CompilerParams(vmem_limit_bytes=VMEM_LIMIT)


def mix_kernel(vertical_ref, basis_ref, member_ref, increment_ref, coeffs_ref, *refs):
    *out_refs, total = refs
    vertical = vertical_ref[...]
    product = jnp.swapaxes(member_ref[...] * increment_ref[...], 0, 1)
    mixed = [
        jnp.dot(vertical, product[p], preferred_element_type=F32).astype(BF16)
        for p in range(product.shape[0])
    ]
    mixed = jnp.swapaxes(jnp.stack(mixed, axis=0), 0, 1)
    parts, start, stored, _ = coeffs_ref.shape
    first = mixed[:start].reshape(start * stored, mixed.shape[-1])
    more = jnp.dot(first, basis_ref[...], preferred_element_type=F32)
    step, last = pl.program_id(0), pl.num_programs(0) - 1

    @pl.when(step == 0)
    def _():
        total[...] = more

    @pl.when((step > 0) & (step < last))
    def _():
        total[...] += more

    @pl.when(step == last)
    def _():
        done = (total[...] + more).astype(BF16)
        for s in range(parts):
            coeffs_ref[s] = done[:, s * LANES : (s + 1) * LANES].reshape(start, stored, LANES)

    for out_ref in out_refs:
        size = out_ref.shape[0]
        out_ref[...] = mixed[start : start + size]
        start += size


def mix(vertical, basis, member, increment, chunks, width=256):
    levels, stored, columns = member.shape
    parts = columns // LANES
    wide = lambda size: pl.BlockSpec((size, stored, width), lambda i: (0, 0, i))
    first = (parts, chunks[0], stored, LANES)
    return pl.pallas_call(
        mix_kernel,
        grid=(columns // width,),
        in_specs=[
            pl.BlockSpec((levels, levels), lambda i: (0, 0)),
            pl.BlockSpec((width, columns), lambda i: (i, 0)),
            wide(levels),
            wide(levels),
        ],
        out_specs=[pl.BlockSpec(first, lambda i: (0, 0, 0, 0))] + [wide(n) for n in chunks[1:]],
        out_shape=[pltpu.HBM(first, BF16)]
        + [pltpu.HBM((n, stored, columns), BF16) for n in chunks[1:]],
        scratch_shapes=[pltpu.VMEM((chunks[0] * stored, columns), F32)],
        compiler_params=pltpu.CompilerParams(vmem_limit_bytes=40 * 1024 * 1024),
        name="mix",
    )(vertical, *[pltpu.with_memory_space_constraint(a, pltpu.HBM) for a in (basis, member, increment)])


def cost(flops, values):
    return pl.CostEstimate(flops=flops, bytes_accessed=2 * values, transcendentals=0)


def at_tile(tile):
    return pl.ds(pl.multiple_of(tile * LANES, LANES), LANES)


def forward_kernel(basis_ref, x_ref, out_ref):
    step, stored, columns = x_ref.shape
    coeffs = jnp.dot(
        x_ref[...].reshape(step * stored, columns), basis_ref[...], preferred_element_type=F32
    ).astype(BF16)
    for d in range(out_ref.shape[0]):
        out_ref[d] = coeffs[:, d * LANES : (d + 1) * LANES].reshape(step, stored, LANES)


def forward(basis, x, at=0):
    size, stored, columns = x.shape
    parts = columns // LANES
    step = min(STEP, size)
    first = at // step
    assert first * step == at
    return pl.pallas_call(
        forward_kernel,
        grid=(pl.cdiv(size, step),),
        in_specs=[
            pl.BlockSpec((columns, columns), lambda i: (0, 0)),
            pl.BlockSpec((step, stored, columns), lambda i: (i, 0, 0)),
        ],
        out_specs=pl.BlockSpec((parts, step, stored, LANES), lambda i: (0, first + i, 0, 0)),
        out_shape=pltpu.HBM((parts, at + size, stored, LANES), BF16),
        compiler_params=params(),
        cost_estimate=cost(2 * x.size * columns, 2 * x.size + basis.size),
        name="forward",
    )(basis, pltpu.with_memory_space_constraint(x, pltpu.HBM))


def filter_kernel(basis_ref, basis_t_ref, weights_ref, x_ref, *refs):
    out_ref = refs[-1]
    parts, step, stored, width = x_ref.shape
    x = jnp.concatenate([x_ref[:, l].reshape(parts * stored, width) for l in range(step)], axis=1)
    spectral = jnp.dot(basis_ref[...], x, preferred_element_type=F32)
    weights = jnp.concatenate([weights_ref[...]] * step, axis=1)
    damped = (spectral * weights).astype(BF16)
    back = jnp.dot(basis_t_ref[...], damped, preferred_element_type=F32).astype(BF16)
    for l in range(step):
        out_ref[:, l] = back[:, l * width : (l + 1) * width].reshape(parts, stored, width)


def filter_rows(basis, basis_t, weights, x, start, size, buffer=None):
    parts, _, stored, width = x.shape
    step = min(SHORT, size)
    first = start // step
    assert first * step == start
    whole = lambda a: pl.BlockSpec(a.shape, lambda i: (0, 0))
    held = [] if buffer is None else [buffer]
    shape = (parts, size, stored, width) if buffer is None else buffer.shape
    total = parts * size * stored * width
    return pl.pallas_call(
        filter_kernel,
        grid=(pl.cdiv(size, step),),
        in_specs=[whole(basis), whole(basis_t), whole(weights)]
        + [pl.BlockSpec((parts, step, stored, width), lambda i: (0, first + i, 0, 0))]
        + [pl.BlockSpec(memory_space=pl.ANY)] * len(held),
        out_specs=pl.BlockSpec((parts, step, stored, width), lambda i: (0, i, 0, 0)),
        out_shape=pltpu.HBM(shape, BF16),
        input_output_aliases={4: 0} if held else {},
        compiler_params=params(),
        cost_estimate=cost(4 * parts * stored * total, 2 * total),
        name="filter",
    )(basis, basis_t, weights, x, *[pltpu.with_memory_space_constraint(a, pltpu.HBM) for a in held])


def backward_kernel(tiles_ref, basis_ref, member_ref, x_ref, keep_ref, give_ref, held):
    parts, step, stored, width = x_ref.shape
    x = jnp.concatenate([x_ref[d].reshape(step * stored, width) for d in range(parts)], axis=1)
    gridded = jnp.dot(x, basis_ref[...], preferred_element_type=F32)
    held[...] = (member_ref[...].astype(F32).reshape(gridded.shape) * gridded).astype(BF16)
    half = parts // 2
    for q in range(half):
        keep_ref[q] = held[:, at_tile(tiles_ref[q])].reshape(step, stored, width)
        give_ref[q] = held[:, at_tile(tiles_ref[half + q])].reshape(step, stored, width)


def backward(tiles, basis, member, x, start, size):
    parts, _, stored, width = x.shape
    columns = parts * width
    step = min(STEP, size)
    first = start // step
    assert first * step == start
    half = pl.BlockSpec((parts // 2, step, stored, width), lambda i, *_: (0, i, 0, 0))
    total = parts * size * stored * width
    return pl.pallas_call(
        backward_kernel,
        grid_spec=pltpu.PrefetchScalarGridSpec(
            num_scalar_prefetch=1,
            grid=(pl.cdiv(size, step),),
            in_specs=[
                pl.BlockSpec((columns, columns), lambda i, *_: (0, 0)),
                pl.BlockSpec((step, stored, columns), lambda i, *_: (first + i, 0, 0)),
                pl.BlockSpec((parts, step, stored, width), lambda i, *_: (0, i, 0, 0)),
            ],
            out_specs=[half] * 2,
            scratch_shapes=[pltpu.VMEM((step * stored, columns), BF16)],
        ),
        out_shape=[jax.ShapeDtypeStruct((parts // 2, size, stored, width), BF16)] * 2,
        compiler_params=params(),
        cost_estimate=cost(2 * total * columns, 3 * total + basis.size),
        name="backward",
    )(tiles, *[pltpu.with_memory_space_constraint(a, pltpu.HBM) for a in (basis, member)], x)


def pair_kernel(a_ref, b_ref, *out_refs):
    for q, out_ref in enumerate(out_refs):
        out_ref[...] = (a_ref[q].astype(F32) + b_ref[q].astype(F32)).astype(BF16)


def pair_sum(a, b):
    parts, size, stored, width = a.shape
    step = min(STEP, size)
    block = pl.BlockSpec((parts, step, stored, width), lambda i: (0, i, 0, 0))
    return pl.pallas_call(
        pair_kernel,
        grid=(pl.cdiv(size, step),),
        in_specs=[block] * 2,
        out_specs=[pl.BlockSpec((step, stored, width), lambda i: (i, 0, 0))] * parts,
        out_shape=[jax.ShapeDtypeStruct(a.shape[1:], BF16)] * parts,
        compiler_params=params(),
        cost_estimate=cost(a.size, 3 * a.size),
        name="pair_sum",
    )(a, b)


def place_kernel(tiles_ref, mine_ref, theirs_ref, *refs):
    out_ref = refs[-1]
    half = mine_ref.shape[0]
    for q in range(half):
        out_ref[:, :, at_tile(tiles_ref[q])] = mine_ref[q]
        out_ref[:, :, at_tile(tiles_ref[half + q])] = theirs_ref[q]


def place(tiles, mine, theirs, out, start, levels):
    half, size, stored, width = mine.shape
    columns = 2 * half * width
    step = min(STEP, size)
    first = start // step
    block = pl.BlockSpec((half, step, stored, width), lambda i, *_: (0, i, 0, 0))
    held = [] if out is None else [out]
    return pl.pallas_call(
        place_kernel,
        grid_spec=pltpu.PrefetchScalarGridSpec(
            num_scalar_prefetch=1,
            grid=(pl.cdiv(size, step),),
            in_specs=[block] * 2 + [pl.BlockSpec(memory_space=pl.ANY)] * len(held),
            out_specs=pl.BlockSpec((step, stored, columns), lambda i, *_: (first + i, 0, 0)),
        ),
        out_shape=jax.ShapeDtypeStruct((levels, stored, columns), BF16),
        input_output_aliases={3: 0} if held else {},
        compiler_params=params(),
        cost_estimate=cost(0, 4 * mine.size),
        name="place",
    )(tiles, mine, theirs, *held)


Y, XLO, CORE, Z, XHI = 4, 2, 2, 4, 2


def space_to(dz, dx):
    return [(z * XHI + x, (z + dz) % Z * XHI + (x ^ dx)) for z in range(Z) for x in range(XHI)]


def mem_to(dy, dx, dc):
    return [
        ((y * XLO + x) * CORE + c, ((y + dy) % Y * XLO + (x ^ dx)) * CORE + (c ^ dc))
        for y in range(Y)
        for x in range(XLO)
        for c in range(CORE)
    ]


def swap(pieces):
    return lax.all_to_all(pieces, "space", 0, 0, tiled=True)


tie = lax.optimization_barrier


def add(*terms):
    return sum(t.astype(F32) for t in terms).astype(BF16)


def shards(members, increment, vertical, spectral_weights, tile_rows):
    levels, stored, columns = increment.shape
    member = members[0]
    table = wave_table(columns)
    basis_x, basis_xt = jnp.asarray(table), jnp.asarray(np.ascontiguousarray(table.T))
    space, mem = lax.axis_index("space"), lax.axis_index("mem")
    z, x, y, core = space // XHI, space % XHI, mem // (XLO * CORE), mem % CORE
    tiles = jnp.stack(
        [(core ^ dc) * Y + (y + dy) % Y for dc in range(CORE) for dy in range(Y)]
    ).astype(jnp.int32)
    rows = tile_rows.shape[0]
    held = tile_rows[None, :]
    chosen = (lax.broadcasted_iota(jnp.int32, (rows, rows), 0) == held).astype(BF16)
    basis_y = jnp.dot(jnp.asarray(wave_table(rows)), chosen, preferred_element_type=F32).astype(BF16)
    basis_yt = basis_y.T
    localized = mix(vertical, basis_xt, member, increment, CHUNKS)
    starts = [sum(CHUNKS[:i]) for i in range(len(CHUNKS))]

    def spread(i):
        return forward(basis_xt, localized[i], CHUNKS[i - 1])

    def damp(i, came, buffer=None):
        start = CHUNKS[i - 1] if i else 0
        return filter_rows(basis_y, basis_yt, spectral_weights, came, start, CHUNKS[i], buffer)

    def regrid(i, came):
        return backward(tiles, basis_x, member, came, starts[i], CHUNKS[i])

    def fold(keep, give):
        return pair_sum(keep, lax.ppermute(give, "mem", mem_to(0, 0, 1)))

    def scatter(kept):
        return [kept[0]] + [lax.ppermute(kept[dy], "mem", mem_to(dy, 0, 0)) for dy in range(1, Y)]

    def cross(part):
        return lax.ppermute(part, "mem", mem_to(0, 1, 0))

    def collect(part):
        return [part] + [lax.ppermute(part, "mem", mem_to(-dy, 0, 0)) for dy in range(1, Y)]

    def give(parts):
        mine = jnp.stack(parts)
        return mine, lax.ppermute(mine, "mem", mem_to(0, 0, 1))

    def along_y(keep):
        part = add(*scatter(keep))
        return add(part, cross(part))

    came = swap(localized[0])
    buffer = spread(1)
    came, buffer = tie((came, buffer))
    came = swap(damp(0, came, buffer))
    buffer = spread(2)
    came, buffer = tie((came, buffer))
    next_came = swap(damp(1, came, buffer))
    half0 = fold(*regrid(0, came))
    sum0 = along_y(half0)
    came, sum0 = tie((next_came, sum0))
    last = swap(damp(2, came))
    half1 = fold(*regrid(1, came))
    done0 = give(collect(sum0))
    last, half1, done0 = tie((last, half1, done0))
    half2 = fold(*regrid(2, last))
    done1 = give(collect(along_y(half1)))
    done2 = collect(along_y(half2))
    out = place(tiles, *done0, None, starts[0], levels)
    done2, out = tie((done2, out))
    out = place(tiles, *done1, out, starts[1], levels)
    return place(tiles, *give(done2), out, starts[2], levels)


def solution(mesh):
    return jax.shard_map(
        shards,
        mesh=mesh,
        in_specs=(
            P("mem", None, "space", None),
            P(None, "space", None),
            P(),
            P(None, "space"),
            P(),
        ),
        out_specs=P(None, "space", None),
        check_vma=False,
    )
```
